32 devices in a mesh: col: 16 (over z, x, core), row: 2 (over y).
Axes of the slice: x: 2, y: 2, z: 4, core: 2. Of those that a mesh axis runs over, the one named last changes fastest.
Arguments:
- start_field: float32 [2, 128, 4096], P(None, 'row', 'col'), may hold values from -36 to 36
- seam_target: float32 [2, 2, 4, 32768], P(None, None, 'row', 'col'), may hold values from -6 to 6
- seam_rows: int32 [4, 4, 32768], P(None, 'row', 'col'), may hold values from 0 to 30
- seam_band: int32 [4, 4, 32768], P(None, 'row', 'col'), may hold values from 0 to 2
- seam_frac: int32 [4, 2, 4, 32768], P(None, None, 'row', 'col'), may hold values from 0 to 255
- adjacency: int32 [2, 4, 128], P(None, 'row', 'col'), may hold values 0 or 1
Outputs:
- refined_field: float32 [2, 128, 4096], P(None, 'row', 'col')
- last_residual: float32 [2, 128, 4096], P(None, 'row', 'col')
The draws below stay inside these ranges and needn't reach their ends.
Inputs may be any that keep to these rules, and one draw needn't show every extreme that they name: `seam_rows`: index of the cell along the seam, in control points of the tile. `seam_band`: depth of the cell from the tile's edge. `seam_frac`: offsets in 256ths of a cell.
All inputs are finite; a program needn't handle non-finite values. No bound on the sum of `adjacency` on one device may be relied on, other than what follows from the above.
Results may differ from the reference program's by a relative error of at most 0.0003.
Values sent between devices are 32-bit elements; how exact they have to be, the bound alone decides.
No kernel may reach another device: no remote copies, remote signals or barrier semaphores. Data moves between devices by JAX's collectives and lax.ppermute only.
A program may use at most 64 MiB of HBM per device.

```python
import jax
import jax.numpy as jnp

GRID = 32
BAND = 4
SAMPLES = 256
ITERS = 3
OUTER = 1
MONT_ROWS = 4
MONT_COLS = 128
HEIGHT = 128
BREADTH = 4096
SEAM_COLS = 32768


def draw_start_field(key, part):
    noise_key, tile_key = jax.random.split(jax.random.fold_in(key, 11))
    tile_scale = jnp.exp(jnp.log(10.0) * jax.random.uniform(tile_key, (MONT_ROWS, MONT_COLS), jnp.float32))
    row_ramp = jnp.arange(MONT_ROWS, dtype=jnp.float32) / max(MONT_ROWS - 1, 1)
    col_ramp = jnp.arange(MONT_COLS, dtype=jnp.float32) / max(MONT_COLS - 1, 1)
    ramp = 1.0 + row_ramp[:, None] + col_ramp[None, :]
    scale = 0.2 * tile_scale * ramp
    cells = jnp.repeat(jnp.repeat(scale, GRID, axis=0), GRID, axis=1)
    noise = jnp.clip(jax.random.normal(noise_key, (2, HEIGHT, BREADTH), jnp.float32), -5.5, 5.5)
    return (noise * cells[None]).astype(jnp.float32)


def touch_ends(entries, rng, low, largest):
    longest = entries.shape.index(max(entries.shape))
    spots = []
    for shift in (0, 1):
        where = [jax.random.randint(jax.random.fold_in(rng, axis), (), 0, length) for axis, length in enumerate(entries.shape)]
        where[longest] = (where[longest] + shift) % entries.shape[longest]
        spots.append(tuple(where))
    return entries.at[spots[0]].set(low).at[spots[1]].set(largest)


def block_scale(own_key, shape, cuts, least, high):
    factor_of, own = 1.0, jax.random.fold_in(own_key, 6)
    for axis_at, shards_of in cuts:
        draws = jnp.exp(jax.random.uniform(jax.random.fold_in(own, axis_at), (shards_of,), jnp.float32, least / len(cuts), high / len(cuts)))
        factor_of = factor_of * jnp.repeat(draws, shape[axis_at] // shards_of).reshape([-1 if axis == axis_at else 1 for axis in range(len(shape))])
    return factor_of


def normal_values(own_key, dims, spread, limit, pieces=(), held_as=jnp.bfloat16):
    gain = block_scale(own_key, dims, pieces, -0.22, 0.18) if pieces else 1.0
    drawn = jax.random.normal(own_key, dims, jnp.float32) * spread * gain
    return jnp.minimum(jnp.maximum(drawn, -limit), limit).astype(held_as)


def setup_inputs(seed: int = 0) -> dict:
    arg_keys = jax.random.split(jax.random.key(seed), 7)
    start_field = draw_start_field(jax.random.fold_in(arg_keys[6], 71), 0)
    seam_target = normal_values(arg_keys[1], (2, 2, MONT_ROWS, SEAM_COLS), 1.0, 6.0, ((2, 2), (3, 16)), jnp.float32)
    seam_rows = touch_ends(jax.random.randint(arg_keys[2], (4, MONT_ROWS, SEAM_COLS), 0, GRID - 1), jax.random.fold_in(arg_keys[2], 1), 0, (GRID - 1) - 1).astype(jnp.int32)
    seam_band = touch_ends(jax.random.randint(arg_keys[3], (4, MONT_ROWS, SEAM_COLS), 0, BAND - 1), jax.random.fold_in(arg_keys[3], 1), 0, (BAND - 1) - 1).astype(jnp.int32)
    seam_frac = touch_ends(jax.random.randint(arg_keys[4], (4, 2, MONT_ROWS, SEAM_COLS), 0, 256), jax.random.fold_in(arg_keys[4], 1), 0, 255).astype(jnp.int32)
    adjacency = touch_ends((jax.random.randint(arg_keys[5], (2, MONT_ROWS, MONT_COLS), 0, 8) < 7).astype(jnp.int32), jax.random.fold_in(arg_keys[5], 1), 0, 1)
    return {"start_field": start_field, "seam_target": seam_target, "seam_rows": seam_rows, "seam_band": seam_band, "seam_frac": seam_frac, "adjacency": adjacency}


BEND_WEIGHT = 0.05
DAMPING = 0.5

def tile_view(control, tile_rows, tile_cols, points):
    return control.reshape(2, tile_rows, points, tile_cols, points)

def edge_band(tile_grid, facing, band_depth):
    if facing == 0:
        return tile_grid[..., ::-1][..., :band_depth].transpose(0, 1, 3, 2, 4)
    if facing == 1:
        return tile_grid[..., :band_depth].transpose(0, 1, 3, 2, 4)
    if facing == 2:
        return tile_grid[:, :, ::-1][:, :, :band_depth].transpose(0, 1, 3, 4, 2)
    return tile_grid[:, :, :band_depth].transpose(0, 1, 3, 4, 2)

def place_edge(band_part, facing, points):
    band_depth = band_part.shape[4]
    if facing < 2:
        widened = jnp.pad(band_part.transpose(0, 1, 3, 2, 4), ((0, 0), (0, 0), (0, 0), (0, 0), (0, points - band_depth)))
        if facing == 0:
            return widened[..., ::-1]
        return widened
    widened = jnp.pad(band_part.transpose(0, 1, 4, 2, 3), ((0, 0), (0, 0), (0, points - band_depth), (0, 0), (0, 0)))
    if facing == 2:
        return widened[:, :, ::-1]
    return widened

def make_tables(along_cell, across, frac_pair):
    weight_along = (frac_pair[0].astype(jnp.float32) + 0.5) / 256.0
    weight_across = (frac_pair[1].astype(jnp.float32) + 0.5) / 256.0
    return (along_cell, across, weight_along, weight_across)

def interpolate(band_part, tables):
    along_cell, across, weight_along, weight_across = tables
    band_depth = band_part.shape[4]
    flattened = band_part.reshape(band_part.shape[:3] + (band_part.shape[3] * band_depth,))
    base_index = (along_cell * band_depth + across).astype(jnp.int32)

    def sample_at(offset):
        gather_index = jnp.broadcast_to((base_index + offset)[None], (2,) + base_index.shape)
        return jnp.take_along_axis(flattened, gather_index, axis=3)
    near = (1.0 - weight_across) * sample_at(0) + weight_across * sample_at(1)
    far_side = (1.0 - weight_across) * sample_at(band_depth) + weight_across * sample_at(band_depth + 1)
    return (1.0 - weight_along) * near + weight_along * far_side

def spread_back(residual, tables, points, band_depth):
    blank_band = jnp.zeros(residual.shape[:3] + (points, band_depth), jnp.float32)
    _, pullback = jax.vjp(lambda band_part: interpolate(band_part, tables), blank_band)
    return pullback(residual)[0]

def bending(control, tile_rows, tile_cols):
    grid_view = tile_view(control, tile_rows, tile_cols, GRID)
    inner = grid_view[:, :, :-2, :, 1:-1] + grid_view[:, :, 2:, :, 1:-1] + grid_view[:, :, 1:-1, :, :-2] + grid_view[:, :, 1:-1, :, 2:] - 4.0 * grid_view[:, :, 1:-1, :, 1:-1]
    widths = ((0, 0), (0, 0), (1, 1), (0, 0), (1, 1))
    curvature = jnp.pad(inner, widths)
    padded = jnp.pad(curvature, widths)
    result = padded[:, :, :-2, :, 1:-1] + padded[:, :, 2:, :, 1:-1] + padded[:, :, 1:-1, :, :-2] + padded[:, :, 1:-1, :, 2:] - 4.0 * curvature
    return result.reshape(control.shape)

def seam_global(control, target, tables, adjacency):
    tile_rows, tile_cols = (adjacency.shape[1], adjacency.shape[2])
    grid_view = tile_view(control, tile_rows, tile_cols, GRID)
    edge_parts = [edge_band(grid_view, facing, BAND) for facing in range(4)]
    seam_values = [interpolate(edge_parts[facing], tables[facing]) for facing in range(4)]
    mask_east = adjacency[0].astype(jnp.float32) * (jnp.arange(tile_cols) < tile_cols - 1).astype(jnp.float32)[None, :]
    mask_south = adjacency[1].astype(jnp.float32) * (jnp.arange(tile_rows) < tile_rows - 1).astype(jnp.float32)[:, None]
    own_east = seam_values[0]
    own_south = seam_values[2]
    if target is not None:
        own_east = own_east - target[0]
        own_south = own_south - target[1]
    blank_col = jnp.zeros((2, tile_rows, 1, SAMPLES), jnp.float32)
    blank_row = jnp.zeros((2, 1, tile_cols, SAMPLES), jnp.float32)
    west_next = jnp.concatenate([seam_values[1][:, :, 1:], blank_col], axis=2)
    north_next = jnp.concatenate([seam_values[3][:, 1:], blank_row], axis=1)
    resid_east = (own_east - west_next) * mask_east[None, :, :, None]
    resid_south = (own_south - north_next) * mask_south[None, :, :, None]
    resid_west = -jnp.concatenate([blank_col, resid_east[:, :, :-1]], axis=2)
    resid_north = -jnp.concatenate([blank_row, resid_south[:, :-1]], axis=1)
    residuals = [resid_east, resid_west, resid_south, resid_north]
    placed = [place_edge(spread_back(residuals[facing], tables[facing], GRID, BAND), facing, GRID) for facing in range(4)]
    summed = placed[0] + placed[1] + placed[2] + placed[3]
    return summed.reshape(control.shape)

def hessian_apply(control, tables, adjacency):
    tile_rows, tile_cols = (adjacency.shape[1], adjacency.shape[2])
    return seam_global(control, None, tables, adjacency) + BEND_WEIGHT * bending(control, tile_rows, tile_cols) + DAMPING * control

def reference(start_field, seam_target, seam_rows, seam_band, seam_frac, adjacency):
    tile_rows, tile_cols = (adjacency.shape[1], adjacency.shape[2])
    along_cells = seam_rows.reshape(4, tile_rows, tile_cols, SAMPLES)
    across_cells = seam_band.reshape(4, tile_rows, tile_cols, SAMPLES)
    frac_cells = seam_frac.reshape(4, 2, tile_rows, tile_cols, SAMPLES)
    tables = [make_tables(along_cells[facing], across_cells[facing], frac_cells[facing]) for facing in range(4)]
    target_cells = seam_target.reshape(2, 2, tile_rows, tile_cols, SAMPLES)
    target = (target_cells[0], target_cells[1])
    control = start_field
    residual = start_field
    for outer_step in range(OUTER):
        gradient = seam_global(control, target, tables, adjacency) + BEND_WEIGHT * bending(control, tile_rows, tile_cols)
        residual = -gradient
        direction = residual
        update = jnp.zeros_like(control)
        norm_now = jnp.sum(residual * residual)
        for iteration in range(ITERS):
            hess_image = hessian_apply(direction, tables, adjacency)
            step_size = norm_now / jnp.sum(direction * hess_image)
            update = update + step_size * direction
            residual = residual - step_size * hess_image
            norm_next = jnp.sum(residual * residual)
            direction = residual + norm_next / norm_now * direction
            norm_now = norm_next
        control = control + update
    return (control, residual)
```

```python
import jax
import jax.numpy as jnp
from jax import lax
from jax.experimental import pallas as pl
from jax.experimental.pallas import tpu as pltpu
from jax.sharding import PartitionSpec as P

GRID = 32
BAND = 4
ITERS = 3
BEND_WEIGHT = 0.05
DAMPING = 0.5

SAMPLES = 256
LANES = 128
PACK = LANES // GRID
TILE_ROWS = 2
HALF_COLS = 4
PIECES = 3
WINDOW_COLS = PIECES * HALF_COLS
WIDTH = WINDOW_COLS * GRID
BLOCK_ROWS = TILE_ROWS * GRID
TABLE_ROWS = 32
HALF_ROWS = BLOCK_ROWS + HALF_COLS * TABLE_ROWS
BOUNDS = WINDOW_COLS - 1

LOW, HIGH = 0.5, 6.0
CENTRE, RADIUS = (HIGH + LOW) / 2, (HIGH - LOW) / 2

BASIS = ITERS + 1
PAIRS = [(i, j) for i in range(BASIS) for j in range(i, BASIS)]
SUM_ROWS = 16

F32, BF16 = jnp.float32, jnp.bfloat16


def hat(offset):
    return jnp.maximum(1.0 - jnp.abs(offset), 0.0)


def pack_kernel(adjacency, field, target, rows, band, frac, own, ahead, back):
    part = lax.axis_index("row") % 2
    not_last_col = (lax.axis_index("col") < lax.axis_size("col") - 1).astype(jnp.int32)
    not_last_row = (lax.axis_index("row") < lax.axis_size("row") - 1).astype(jnp.int32)
    tiles = 2 * HALF_COLS
    sub = lax.broadcasted_iota(jnp.int32, (8, SAMPLES), 0)
    for half in range(2):
        for comp in range(2):
            own[half, :BLOCK_ROWS, comp * LANES : (comp + 1) * LANES] = field[
                comp, :, half * LANES : (half + 1) * LANES
            ]
    for facing in range(4):
        along = rows[facing].astype(F32) + (frac[facing, 0].astype(F32) + 0.5) / 256.0
        across = band[facing].astype(F32) + (frac[facing, 1].astype(F32) + 0.5) / 256.0
        for tile in range(tiles):
            half, base = tile // HALF_COLS, BLOCK_ROWS + tile % HALF_COLS * TABLE_ROWS + 2 * facing
            lanes = slice(tile * SAMPLES, (tile + 1) * SAMPLES)
            own[half, base : base + 2, :] = along[:, lanes]
            own[half, base + 8 : base + 10, :] = across[:, lanes]
            own[half, base + 16 : base + 18, :] = target[facing // 2, facing % 2][:, lanes]
    for tile in range(tiles):
        half, base = tile // HALF_COLS, BLOCK_ROWS + tile % HALF_COLS * TABLE_ROWS + 24
        masks = jnp.zeros((8, SAMPLES), F32)
        for side in range(2):
            for row in range(TILE_ROWS):
                value = adjacency[side, row, tile]
                if side == 0 and tile == tiles - 1:
                    value = value * not_last_col
                if side == 1 and row == TILE_ROWS - 1:
                    value = value * not_last_row
                masks = jnp.where(sub == 2 * side + row, value.astype(F32), masks)
        own[half, base : base + 8, :] = masks
    ahead[...] = own[1 - part]
    back[...] = own[part]


def split(value):
    high = value.astype(BF16)
    return high, (value - high.astype(F32)).astype(BF16)


def window_kernel(pairs, *refs):
    count = 4 * pairs
    pieces = refs[:count]
    mine, theirs, sums, slots, vecs, weight_hi, weight_lo, cross, shift, flipped, spread, sems = refs[count:]
    tile_rows = 4 * pairs
    own_pair = pairs // 2
    part = lax.axis_index("row") % 2

    copies = []
    for pair in range(pairs):
        places = (
            slots.at[2 * pair + part, pl.ds(1 - part, 2)],
            slots.at[2 * pair + 1 - part, pl.ds(1 - part, 2)],
            slots.at[2 * pair + part, 2 * part],
            slots.at[2 * pair + 1 - part, 2 * part],
        )
        for kind in range(4):
            at = 4 * pair + kind
            copies.append(pltpu.make_async_copy(pieces[at], places[kind], sems.at[at]))
    for copy in copies:
        copy.start()
    for copy in copies:
        copy.wait()

    sub8 = lax.broadcasted_iota(jnp.int32, (8, LANES), 0)
    lane8 = lax.broadcasted_iota(jnp.int32, (8, LANES), 1)
    near_side = sub8 >= 4
    sub16 = lax.broadcasted_iota(jnp.int32, (16, 2 * LANES), 0)
    lane16 = lax.broadcasted_iota(jnp.int32, (16, 2 * LANES), 1)
    side16 = (lane16 < LANES) == (sub16 % 8 >= 4)
    keep = [
        jnp.where(side16 & (lane16 % LANES // GRID == unit), 1.0, 0.0).astype(BF16)
        for unit in range(PACK)
    ]

    for block in range(2 * pairs):
        for piece in range(PIECES):
            for comp in range(2):
                vecs[0, comp, block * BLOCK_ROWS : (block + 1) * BLOCK_ROWS, piece * LANES : (piece + 1) * LANES] = slots[
                    block, piece, :BLOCK_ROWS, comp * LANES : (comp + 1) * LANES
                ]

    def table(row, col, entry):
        start = BLOCK_ROWS + col % HALF_COLS * TABLE_ROWS + entry
        return slots[row // TILE_ROWS, col // HALF_COLS, start : start + 1, :]

    along_iota = lax.broadcasted_iota(jnp.int32, (GRID, SAMPLES), 0).astype(F32)
    sub_s = lax.broadcasted_iota(jnp.int32, (8, SAMPLES), 0)
    near_s = sub_s >= 4
    depth = jnp.where(near_s, 7 - sub_s, sub_s).astype(F32)

    def east_group(bound, group):
        return bound * pairs + group

    def south_group(row, group):
        return BOUNDS * pairs + row * PIECES + group

    def set_tables(index, direction, near_tiles, far_tiles):
        for unit in range(PACK):
            both = (near_tiles[unit], far_tiles[unit])
            ys = []
            for side in range(2):
                row, col = both[side]
                entry = 2 * (2 * direction + side) + row % TILE_ROWS
                weight = hat(table(row, col, entry) - along_iota)
                high, low = split(weight)
                start = side * LANES + unit * GRID
                weight_hi[index, start : start + GRID, :] = high
                weight_lo[index, start : start + GRID, :] = low
                ys.append(table(row, col, 8 + entry))
            row, col = both[0]
            mask = table(row, col, 24 + 2 * direction + row % TILE_ROWS)
            signed = jnp.where(near_s, mask, -mask)
            cross[index, 8 * unit : 8 * unit + 8, :] = hat(jnp.where(near_s, ys[0], ys[1]) - depth) * signed
            for comp in range(2):
                shift[index, 2 * unit + comp : 2 * unit + comp + 1, :] = table(
                    row, col, 16 + 4 * direction + 2 * comp + row % TILE_ROWS
                )

    for bound in range(BOUNDS):
        for group in range(pairs):
            tiles = [(4 * group + unit, bound) for unit in range(PACK)]
            set_tables(east_group(bound, group), 0, tiles, [(row, col + 1) for row, col in tiles])
    for row in range(tile_rows - 1):
        for group in range(PIECES):
            tiles = [(row, 4 * group + unit) for unit in range(PACK)]
            set_tables(south_group(row, group), 1, tiles, [(at + 1, col) for at, col in tiles])

    spread[...] = jnp.zeros_like(spread)

    def seam_group(index, strips, first):
        high, low = split(jnp.concatenate(strips, axis=0))
        high = jnp.concatenate([high, high], axis=1)
        low = jnp.concatenate([low, low], axis=1)
        left_hi = jnp.concatenate([high * keep[unit] for unit in range(PACK)], axis=0)
        left_lo = jnp.concatenate([low * keep[unit] for unit in range(PACK)], axis=0)
        w_hi, w_lo = weight_hi[index], weight_lo[index]
        gathered = (
            jnp.dot(left_hi, w_hi, preferred_element_type=F32)
            + jnp.dot(left_lo, w_hi, preferred_element_type=F32)
            + jnp.dot(left_hi, w_lo, preferred_element_type=F32)
        )
        pulled = []
        for unit in range(PACK):
            across = cross[index, 8 * unit : 8 * unit + 8, :]
            for comp in range(2):
                at = 2 * unit + comp
                total = jnp.sum(gathered[8 * at : 8 * at + 8] * across, axis=0, keepdims=True)
                if first:
                    total = total - shift[index, at : at + 1, :]
                pulled.append(total * across)
        right_hi, right_lo = split(jnp.concatenate(pulled, axis=0))
        numbers = (((1,), (1,)), ((), ()))
        back = (
            lax.dot_general(right_hi, w_hi, numbers, preferred_element_type=F32)
            + lax.dot_general(right_lo, w_hi, numbers, preferred_element_type=F32)
            + lax.dot_general(right_hi, w_lo, numbers, preferred_element_type=F32)
        )
        result = []
        for comp in range(2):
            out = None
            for unit in range(PACK):
                at = 8 * (2 * unit + comp)
                chosen = jnp.where(near_side, back[at : at + 8, :LANES], back[at : at + 8, LANES:])
                out = chosen if out is None else jnp.where(lane8 // GRID == unit, chosen, out)
            result.append(out)
        return result

    sub32 = lax.broadcasted_iota(jnp.int32, (GRID, LANES), 0)
    lane32 = lax.broadcasted_iota(jnp.int32, (GRID, LANES), 1) % GRID
    inner = (sub32 >= 1) & (sub32 <= GRID - 2) & (lane32 >= 1) & (lane32 <= GRID - 2)

    def laplacian(value):
        return (
            pltpu.roll(value, 1, 0)
            + pltpu.roll(value, GRID - 1, 0)
            + pltpu.roll(value, 1, 1)
            + pltpu.roll(value, LANES - 1, 1)
            - 4.0 * value
        )

    def apply(step, scale, own_weight, last_weight):
        for comp in range(2):
            for group in range(pairs):
                for piece in range(PIECES):
                    flipped[comp, piece * LANES : (piece + 1) * LANES, group * LANES : (group + 1) * LANES] = vecs[
                        step, comp, group * LANES : (group + 1) * LANES, piece * LANES : (piece + 1) * LANES
                    ].T
        for bound in range(step, BOUNDS - step):
            at = GRID * bound + GRID - 8
            for group in range(pairs):
                lanes = slice(group * LANES, (group + 1) * LANES)
                strips = [
                    jnp.where(near_side, flipped[comp, at : at + 8, lanes], flipped[comp, at + 8 : at + 16, lanes])
                    for comp in range(2)
                ]
                result = seam_group(east_group(bound, group), strips, step == 0)
                for comp in range(2):
                    spread[comp, at : at + 8, lanes] = jnp.where(near_side, result[comp], 0.0)
                    spread[comp, at + 8 : at + 16, lanes] = jnp.where(near_side, 0.0, result[comp])
        used = (1,) if step == ITERS else range(PIECES)
        for piece in used:
            lanes = slice(piece * LANES, (piece + 1) * LANES)
            for comp in range(2):
                for group in range(pairs):
                    turned = spread[comp, lanes, group * LANES : (group + 1) * LANES].T
                    for unit in range(PACK):
                        start = group * LANES + unit * GRID
                        value = vecs[step, comp, start : start + GRID, lanes]
                        curved = laplacian(jnp.where(inner, laplacian(value), 0.0))
                        out = scale * (turned[unit * GRID : (unit + 1) * GRID] + BEND_WEIGHT * curved)
                        if own_weight:
                            out = out + own_weight * value
                        if last_weight:
                            out = out + last_weight * vecs[step - 1, comp, start : start + GRID, lanes]
                        vecs[step + 1, comp, start : start + GRID, lanes] = out
            for row in range(tile_rows - 1):
                at = GRID * row + GRID - 8
                strips = [
                    jnp.where(near_side, vecs[step, comp, at : at + 8, lanes], vecs[step, comp, at + 8 : at + 16, lanes])
                    for comp in range(2)
                ]
                result = seam_group(south_group(row, piece), strips, step == 0)
                for comp in range(2):
                    vecs[step + 1, comp, at : at + 8, lanes] += jnp.where(near_side, scale * result[comp], 0.0)
                    vecs[step + 1, comp, at + 8 : at + 16, lanes] += jnp.where(near_side, 0.0, scale * result[comp])

    apply(0, -1.0, 0.0, 0.0)
    apply(1, 1.0 / RADIUS, (DAMPING - CENTRE) / RADIUS, 0.0)
    apply(2, 2.0 / RADIUS, 2.0 * (DAMPING - CENTRE) / RADIUS, -1.0)
    apply(3, 2.0 / RADIUS, 2.0 * (DAMPING - CENTRE) / RADIUS, -1.0)

    first_row = own_pair * 2 * BLOCK_ROWS
    partial = [jnp.zeros((8, LANES), F32) for _ in PAIRS]
    for comp in range(2):
        for row in range(first_row, first_row + 2 * BLOCK_ROWS, 8):
            values = [vecs[1 + k, comp, row : row + 8, LANES : 2 * LANES] for k in range(BASIS)]
            for n, (i, j) in enumerate(PAIRS):
                partial[n] = partial[n] + values[i] * values[j]
    rows = [jnp.sum(value, axis=0, keepdims=True) for value in partial]
    rows.append(jnp.zeros((SUM_ROWS - len(rows), LANES), F32))
    sums[...] = jnp.concatenate(rows, axis=0)
    for k in range(BASIS):
        for comp in range(2):
            for out, block in ((mine, part), (theirs, 1 - part)):
                start = pl.multiple_of(first_row + block * BLOCK_ROWS, BLOCK_ROWS)
                out[k, comp] = vecs[1 + k, comp, pl.ds(start, BLOCK_ROWS), LANES : 2 * LANES]


def final_kernel(sums, mine, other, field, control, residual):
    part = lax.axis_index("row") % 2
    totals = jnp.sum(sums[...], axis=1, keepdims=True)
    gram = {}
    for n, (i, j) in enumerate(PAIRS):
        gram[i, j] = gram[j, i] = jnp.broadcast_to(totals[n : n + 1], (1, LANES))

    def inner(left, right):
        return sum(
            left[i] * sum(gram[i, j] * right[j] for j in right) for i in left
        )

    def image(vec):
        out = {}

        def add(at, value):
            out[at] = out[at] + value if at in out else value

        for k, value in vec.items():
            add(k, CENTRE * value)
            if k == 0:
                add(1, RADIUS * value)
            else:
                add(k - 1, RADIUS / 2 * value)
                add(k + 1, RADIUS / 2 * value)
        return out

    one = jnp.ones((1, LANES), F32)
    resid, direction, update = {0: one}, {0: one}, {}
    norm = gram[0, 0]
    for iteration in range(ITERS):
        moved = image(direction)
        step = norm / inner(direction, moved)
        for k, value in direction.items():
            update[k] = update[k] + step * value if k in update else step * value
        resid = {k: (resid[k] if k in resid else 0.0) - step * value for k, value in moved.items()}
        if iteration < ITERS - 1:
            after = inner(resid, resid)
            ratio = after / norm
            direction = {k: value + ratio * direction[k] if k in direction else value for k, value in resid.items()}
            norm = after

    for source, half in ((mine, part), (other, 1 - part)):
        lanes = pl.ds(pl.multiple_of(half * LANES, LANES), LANES)
        for comp in range(2):
            basis = [source[k, comp] for k in range(BASIS)]
            control[comp, :, lanes] = field[comp, :, lanes] + sum(update[k] * basis[k] for k in update)
            residual[comp, :, lanes] = sum(resid[k] * basis[k] for k in resid)


def shards(start_field, seam_target, seam_rows, seam_band, seam_frac, adjacency):
    row_count, col_count = lax.axis_size("row"), lax.axis_size("col")
    axes = ("col", "row")
    vmem = pl.BlockSpec(memory_space=pltpu.VMEM)
    anywhere = pl.BlockSpec(memory_space=pl.ANY)
    limit = pltpu.CompilerParams(vmem_limit_bytes=48 * 1024 * 1024)

    def shifted(value, move):
        sources = [(col, row) for col in range(col_count) for row in range(row_count)]
        perm = []
        for col, row in sources:
            to_col, to_row = move(col, row)
            if 0 <= to_col < col_count and 0 <= to_row < row_count:
                perm.append((col * row_count + row, to_col * row_count + to_row))
        return lax.ppermute(value, axes, perm)

    half = jax.ShapeDtypeStruct((HALF_ROWS, SAMPLES), F32)
    own, ahead, back = pl.pallas_call(
        pack_kernel,
        out_shape=(jax.ShapeDtypeStruct((2, HALF_ROWS, SAMPLES), F32), half, half),
        in_specs=[pl.BlockSpec(memory_space=pltpu.SMEM)] + [vmem] * 5,
        out_specs=(vmem, vmem, vmem),
        name="pack",
    )(adjacency, start_field, seam_target, seam_rows, seam_band, seam_frac)

    outward = lambda row: 1 - 2 * (row % 2)
    pieces = (
        own,
        shifted(own, lambda col, row: (col, row ^ 1)),
        shifted(ahead, lambda col, row: (col + outward(row), row)),
        shifted(back, lambda col, row: (col - outward(row), row ^ 1)),
    )
    if row_count > 2:
        from_above = [shifted(piece, lambda col, row: (col, row + 2)) for piece in pieces]
        from_below = [shifted(piece, lambda col, row: (col, row - 2)) for piece in pieces]
        pieces = (*from_above, *pieces, *from_below)
    pairs = len(pieces) // 4
    groups = BOUNDS * pairs + (4 * pairs - 1) * PIECES

    part_shape = jax.ShapeDtypeStruct((BASIS, 2, BLOCK_ROWS, LANES), F32)
    mine, theirs, sums = pl.pallas_call(
        lambda *refs: window_kernel(pairs, *refs),
        out_shape=(part_shape, part_shape, jax.ShapeDtypeStruct((SUM_ROWS, LANES), F32)),
        in_specs=[anywhere] * len(pieces),
        out_specs=(vmem, vmem, vmem),
        scratch_shapes=[
            pltpu.VMEM((2 * pairs, PIECES, HALF_ROWS, SAMPLES), F32),
            pltpu.VMEM((BASIS + 1, 2, 4 * pairs * GRID, WIDTH), F32),
            pltpu.VMEM((groups, 2 * LANES, SAMPLES), BF16),
            pltpu.VMEM((groups, 2 * LANES, SAMPLES), BF16),
            pltpu.VMEM((groups, 8 * PACK, SAMPLES), F32),
            pltpu.VMEM((groups, 2 * PACK, SAMPLES), F32),
            pltpu.VMEM((2, WIDTH, pairs * LANES), F32),
            pltpu.VMEM((2, WIDTH, pairs * LANES), F32),
            pltpu.SemaphoreType.DMA((len(pieces),)),
        ],
        compiler_params=limit,
        name="window",
    )(*pieces)

    other = shifted(theirs, lambda col, row: (col, row ^ 1))
    for axis, size in (("col", col_count), ("row", row_count)):
        if size & (size - 1):
            sums = lax.psum(sums, axis)
            continue
        hop = 1
        while hop < size:
            sums = sums + lax.ppermute(sums, axis, [(at, at ^ hop) for at in range(size)])
            hop *= 2

    out = jax.ShapeDtypeStruct(start_field.shape, F32)
    return pl.pallas_call(
        final_kernel,
        out_shape=(out, out),
        in_specs=[vmem] * 4,
        out_specs=(vmem, vmem),
        name="final",
    )(sums, mine, other, start_field)


def solution(mesh):
    placed = (
        P(None, "row", "col"),
        P(None, None, "row", "col"),
        P(None, "row", "col"),
        P(None, "row", "col"),
        P(None, None, "row", "col"),
        P(None, "row", "col"),
    )
    return jax.shard_map(
        shards,
        mesh=mesh,
        in_specs=placed,
        out_specs=(P(None, "row", "col"), P(None, "row", "col")),
        check_vma=False,
    )
```

```python
import jax
import jax.numpy as jnp
from jax import lax
from jax.experimental import pallas as pl
from jax.experimental.pallas import tpu as pltpu
from jax.sharding import PartitionSpec as P

GRID = 32
BAND = 4
ITERS = 3
BEND_WEIGHT = 0.05
DAMPING = 0.5

SAMPLES = 256
LANES = 128
PACK = LANES // GRID
TILE_ROWS = 2
HALF_COLS = 4
PIECES = 3
WINDOW_COLS = PIECES * HALF_COLS
WIDTH = WINDOW_COLS * GRID
BLOCK_ROWS = TILE_ROWS * GRID
MASK_ROWS = 8
MASK_LANES = SAMPLES // HALF_COLS
TABLE_ROWS = 24
TABLES = BLOCK_ROWS + MASK_ROWS
HALF_ROWS = TABLES + HALF_COLS * TABLE_ROWS
BOUNDS = WINDOW_COLS - 1

LOW, HIGH = 0.5, 6.0
CENTRE, RADIUS = (HIGH + LOW) / 2, (HIGH - LOW) / 2

BASIS = ITERS + 1
PAIRS = [(i, j) for i in range(BASIS) for j in range(i, BASIS)]
SUM_ROWS = 16
SUM_LANES = LANES // SUM_ROWS
EDGE = 8

F32, BF16 = jnp.float32, jnp.bfloat16


def hat(offset):
    return jnp.maximum(1.0 - jnp.abs(offset), 0.0)


def pack_kernel(adjacency, field, target, rows, band, frac, own, ahead, back):
    part = lax.axis_index("row") % 2
    not_last_col = (lax.axis_index("col") < lax.axis_size("col") - 1).astype(jnp.int32)
    not_last_row = (lax.axis_index("row") < lax.axis_size("row") - 1).astype(jnp.int32)
    tiles = 2 * HALF_COLS
    sub = lax.broadcasted_iota(jnp.int32, (MASK_ROWS, SAMPLES), 0)
    for half in range(2):
        for comp in range(2):
            own[half, :BLOCK_ROWS, comp * LANES : (comp + 1) * LANES] = field[
                comp, :, half * LANES : (half + 1) * LANES
            ]
    for facing in range(4):
        along = rows[facing].astype(F32) + (frac[facing, 0].astype(F32) + 0.5) / 256.0
        across = band[facing].astype(F32) + (frac[facing, 1].astype(F32) + 0.5) / 256.0
        for tile in range(tiles):
            half, base = tile // HALF_COLS, TABLES + tile % HALF_COLS * TABLE_ROWS + 2 * facing
            lanes = slice(tile * SAMPLES, (tile + 1) * SAMPLES)
            own[half, base : base + 2, :] = along[:, lanes]
            own[half, base + 8 : base + 10, :] = across[:, lanes]
            own[half, base + 16 : base + 18, :] = target[facing // 2, facing % 2][:, lanes]
    unit = lax.broadcasted_iota(jnp.int32, (MASK_ROWS, SAMPLES), 1) // MASK_LANES
    for half in range(2):
        masks = jnp.zeros((MASK_ROWS, SAMPLES), F32)
        for tile in range(half * HALF_COLS, (half + 1) * HALF_COLS):
            for side in range(2):
                for row in range(TILE_ROWS):
                    value = adjacency[side, row, tile]
                    if side == 0 and tile == tiles - 1:
                        value = value * not_last_col
                    if side == 1 and row == TILE_ROWS - 1:
                        value = value * not_last_row
                    here = (sub == 2 * side + row) & (unit == tile % HALF_COLS)
                    masks = jnp.where(here, value.astype(F32), masks)
        own[half, BLOCK_ROWS:TABLES, :] = masks
    ahead[...] = own[1 - part]
    back[...] = own[part]


def split(value):
    high = value.astype(BF16)
    return high, (value - high.astype(F32)).astype(BF16)


def groups_of(pairs):
    order, counts = [], []
    for reach in range(ITERS + 1):
        step = ITERS - reach
        for bound in range(step, BOUNDS - step):
            order += [(0, bound, group) for group in range(pairs)]
        for piece in (1,) if step == ITERS else range(PIECES):
            order += [(1, row, piece) for row in range(4 * pairs - 1)]
        order = list(dict.fromkeys(order))
        counts.append(len(order))
    return order, counts[::-1]


def window_kernel(pairs, *refs):
    count = 4 * pairs
    pieces = refs[:count]
    mine, theirs, sums, slots, vecs, weight_hi, weight_lo, turned_hi, turned_lo, cross, shift, *rest = refs[count:]
    strip_in, strip_out, flipped, spread, bends, sems = rest
    order, counts = groups_of(pairs)
    own_pair = pairs // 2
    part = lax.axis_index("row") % 2

    copies = []
    for pair in range(pairs):
        places = (
            slots.at[2 * pair + part, pl.ds(1 - part, 2)],
            slots.at[2 * pair + 1 - part, pl.ds(1 - part, 2)],
            slots.at[2 * pair + part, 2 * part],
            slots.at[2 * pair + 1 - part, 2 * part],
        )
        for kind in range(4):
            at = 4 * pair + kind
            copies.append(pltpu.make_async_copy(pieces[at], places[kind], sems.at[at]))
    for copy in copies:
        copy.start()
    for copy in copies:
        copy.wait()

    sub8 = lax.broadcasted_iota(jnp.int32, (8, LANES), 0)
    lane8 = lax.broadcasted_iota(jnp.int32, (8, LANES), 1)
    near_side = sub8 >= 4
    sub16 = lax.broadcasted_iota(jnp.int32, (16, 2 * LANES), 0)
    lane16 = lax.broadcasted_iota(jnp.int32, (16, 2 * LANES), 1)
    side16 = (lane16 < LANES) == (sub16 % 8 >= 4)
    keep = [
        jnp.where(side16 & (lane16 % LANES // GRID == unit), 1.0, 0.0).astype(BF16)
        for unit in range(PACK)
    ]

    for block in range(2 * pairs):
        for piece in range(PIECES):
            for comp in range(2):
                start = EDGE + block * BLOCK_ROWS
                vecs[0, comp, piece, start : start + BLOCK_ROWS, :] = slots[
                    block, piece, :BLOCK_ROWS, comp * LANES : (comp + 1) * LANES
                ]

    def table(row, col, entry):
        start = TABLES + col % HALF_COLS * TABLE_ROWS + entry
        return slots[row // TILE_ROWS, col // HALF_COLS, start : start + 1, :]

    along_iota = lax.broadcasted_iota(jnp.int32, (GRID, SAMPLES), 0).astype(F32)
    sub_s = lax.broadcasted_iota(jnp.int32, (8, SAMPLES), 0)
    near_s = sub_s >= 4
    depth = jnp.where(near_s, 7 - sub_s, sub_s).astype(F32)

    def set_tables(index, direction, near_tiles, far_tiles):
        hats = []
        for unit in range(PACK):
            both = (near_tiles[unit], far_tiles[unit])
            ys = []
            for side in range(2):
                row, col = both[side]
                entry = 2 * (2 * direction + side) + row % TILE_ROWS
                weight = hat(table(row, col, entry) - along_iota)
                high, low = split(weight)
                start = side * LANES + unit * GRID
                weight_hi[index, start : start + GRID, :] = high
                weight_lo[index, start : start + GRID, :] = low
                hats.append(weight)
                ys.append(table(row, col, 8 + entry))
            row, col = both[0]
            at, lane = BLOCK_ROWS + 2 * direction + row % TILE_ROWS, col % HALF_COLS * MASK_LANES
            mask = slots[row // TILE_ROWS, col // HALF_COLS, at : at + 1, lane : lane + 1]
            signed = jnp.where(near_s, mask, -mask)
            rows = slice(8 * unit, 8 * unit + 8)
            across = hat(jnp.where(near_s, ys[0], ys[1]) - depth) * signed
            cross[index, rows, :] = across
            for comp in range(2):
                shift[index, 2 * unit + comp : 2 * unit + comp + 1, :] = table(
                    row, col, 16 + 4 * direction + 2 * comp + row % TILE_ROWS
                )
        ordered = jnp.concatenate(hats[0::2] + hats[1::2], axis=0).T
        high, low = split(ordered)
        turned_hi[index] = high
        turned_lo[index] = low

    for index, (direction, at, group) in enumerate(order):
        if direction == 0:
            tiles = [(PACK * group + unit, at) for unit in range(PACK)]
            set_tables(index, 0, tiles, [(row, col + 1) for row, col in tiles])
        else:
            tiles = [(at, PACK * group + unit) for unit in range(PACK)]
            set_tables(index, 1, tiles, [(row + 1, col) for row, col in tiles])

    spread[...] = jnp.zeros_like(spread)
    bends[...] = jnp.zeros_like(bends)

    def seam_batch(indices, first):
        half = 8 * 2 * PACK
        gathered = []
        for index in indices:
            high, low = split(jnp.concatenate([strip_in[index, comp] for comp in range(2)], axis=0))
            high = jnp.concatenate([high, high], axis=1)
            low = jnp.concatenate([low, low], axis=1)
            left = jnp.concatenate([high * keep[unit] for unit in range(PACK)] + [low * keep[unit] for unit in range(PACK)], axis=0)
            both = jnp.dot(left, weight_hi[index], preferred_element_type=F32)
            rest = jnp.dot(left[:half], weight_lo[index], preferred_element_type=F32)
            gathered.append(both[:half] + both[half:] + rest)
        pulled = []
        for index, values in zip(indices, gathered):
            parts = []
            for unit in range(PACK):
                across = cross[index, 8 * unit : 8 * unit + 8, :]
                for comp in range(2):
                    at = 2 * unit + comp
                    total = jnp.sum(values[8 * at : 8 * at + 8] * across, axis=0, keepdims=True)
                    if first:
                        total = total - shift[index, at : at + 1, :]
                    parts.append(total * across)
            pulled.append(split(jnp.concatenate(parts, axis=0)))
        numbers = (((1,), (0,)), ((), ()))
        backs = []
        for index, (high, low) in zip(indices, pulled):
            both = lax.dot_general(
                jnp.concatenate([high, low], axis=0), turned_hi[index], numbers, preferred_element_type=F32
            )
            rest = lax.dot_general(high, turned_lo[index], numbers, preferred_element_type=F32)
            backs.append(both[:half] + both[half:] + rest)
        for index, back in zip(indices, backs):
            for comp in range(2):
                out = None
                for unit in range(PACK):
                    at = 8 * (2 * unit + comp)
                    chosen = jnp.where(near_side, back[at : at + 8, :LANES], back[at : at + 8, LANES:])
                    out = chosen if out is None else jnp.where(lane8 // GRID == unit, chosen, out)
                strip_out[index, comp] = out

    sub32 = lax.broadcasted_iota(jnp.int32, (GRID, LANES), 0)
    lane32 = lax.broadcasted_iota(jnp.int32, (GRID, LANES), 1) % GRID
    inner = (sub32 >= 1) & (sub32 <= GRID - 2) & (lane32 >= 1) & (lane32 <= GRID - 2)

    def beside(value):
        return pltpu.roll(value, 1, 1) + pltpu.roll(value, LANES - 1, 1) - 4.0 * value

    def apply(step, scale, own_weight, last_weight):
        for comp in range(2):
            for group in range(pairs):
                for piece in range(PIECES):
                    start = EDGE + group * LANES
                    flipped[comp, piece * LANES : (piece + 1) * LANES, group * LANES : (group + 1) * LANES] = vecs[
                        step, comp, piece, start : start + LANES, :
                    ].T
        used = order[: counts[step]]

        def place(entry):
            direction, at, group = entry
            return GRID * at + GRID - 8, group, slice(group * LANES, (group + 1) * LANES), direction == 0

        for index, entry in enumerate(used):
            at, piece, lanes, east = place(entry)
            for comp in range(2):
                if east:
                    before, after = flipped[comp, at : at + 8, lanes], flipped[comp, at + 8 : at + 16, lanes]
                else:
                    start = EDGE + at
                    before = vecs[step, comp, piece, start : start + 8, :]
                    after = vecs[step, comp, piece, start + 8 : start + 16, :]
                strip_in[index, comp] = jnp.where(near_side, before, after)

        seam_batch(list(range(len(used))), step == 0)

        for index, entry in enumerate(used):
            at, piece, lanes, east = place(entry)
            if east:
                for comp in range(2):
                    spread[comp, at : at + 8, lanes] = jnp.where(near_side, strip_out[index, comp], 0.0)
                    spread[comp, at + 8 : at + 16, lanes] = jnp.where(near_side, 0.0, strip_out[index, comp])
        for piece in (1,) if step == ITERS else range(PIECES):
            for comp in range(2):
                for group in range(pairs):
                    turned = spread[
                        comp, piece * LANES : (piece + 1) * LANES, group * LANES : (group + 1) * LANES
                    ].T
                    for unit in range(PACK):
                        tile = PACK * group + unit
                        start = EDGE + tile * GRID
                        value = vecs[step, comp, piece, start : start + GRID, :]
                        level = jnp.where(
                            inner,
                            vecs[step, comp, piece, start - 1 : start + GRID - 1, :]
                            + vecs[step, comp, piece, start + 1 : start + GRID + 1, :]
                            + beside(value),
                            0.0,
                        )
                        bends[comp, piece, tile, EDGE : EDGE + GRID, :] = level
                        curved = (
                            bends[comp, piece, tile, EDGE - 1 : EDGE + GRID - 1, :]
                            + bends[comp, piece, tile, EDGE + 1 : EDGE + GRID + 1, :]
                            + beside(level)
                        )
                        out = scale * (turned[unit * GRID : (unit + 1) * GRID] + BEND_WEIGHT * curved)
                        if own_weight:
                            out = out + own_weight * value
                        if last_weight:
                            out = out + last_weight * vecs[step - 1, comp, piece, start : start + GRID, :]
                        vecs[step + 1, comp, piece, start : start + GRID, :] = out
        for index, entry in enumerate(used):
            at, piece, lanes, east = place(entry)
            if not east:
                start = EDGE + at
                for comp in range(2):
                    result = scale * strip_out[index, comp]
                    vecs[step + 1, comp, piece, start : start + 8, :] += jnp.where(near_side, result, 0.0)
                    vecs[step + 1, comp, piece, start + 8 : start + 16, :] += jnp.where(near_side, 0.0, result)

    apply(0, -1.0, 0.0, 0.0)
    apply(1, 1.0 / RADIUS, (DAMPING - CENTRE) / RADIUS, 0.0)
    apply(2, 2.0 / RADIUS, 2.0 * (DAMPING - CENTRE) / RADIUS, -1.0)
    apply(3, 2.0 / RADIUS, 2.0 * (DAMPING - CENTRE) / RADIUS, -1.0)

    first_row = EDGE + own_pair * 2 * BLOCK_ROWS
    partial = [jnp.zeros((8, LANES), F32) for _ in PAIRS]
    for comp in range(2):
        for row in range(first_row, first_row + 2 * BLOCK_ROWS, 8):
            values = [vecs[1 + k, comp, 1, row : row + 8, :] for k in range(BASIS)]
            for n, (i, j) in enumerate(PAIRS):
                partial[n] = partial[n] + values[i] * values[j]
    rows = [jnp.sum(value, axis=0, keepdims=True) for value in partial]
    rows.append(jnp.zeros((SUM_ROWS - len(rows), LANES), F32))
    totals = jnp.sum(jnp.concatenate(rows, axis=0), axis=1, keepdims=True)
    slot = lax.broadcasted_iota(jnp.int32, (SUM_ROWS, LANES), 1) // SUM_LANES
    placed = jnp.where(slot == lax.broadcasted_iota(jnp.int32, (SUM_ROWS, LANES), 0), totals, 0.0)
    sums[...] = jnp.broadcast_to(jnp.sum(placed, axis=0, keepdims=True), sums.shape)
    for k in range(BASIS):
        for comp in range(2):
            for out, block in ((mine, part), (theirs, 1 - part)):
                start = pl.multiple_of(first_row + block * BLOCK_ROWS, EDGE)
                out[k, comp] = vecs[1 + k, comp, 1, pl.ds(start, BLOCK_ROWS), :]


def final_kernel(*refs):
    sources, (control, residual), (sums, mine, other, field, sems) = refs[:4], refs[4:6], refs[6:]
    copies = [
        pltpu.make_async_copy(source, target, sems.at[n])
        for n, (source, target) in enumerate(zip(sources, (sums, mine, other, field)))
    ]
    for copy in copies:
        copy.start()
    copies[0].wait()
    part = lax.axis_index("row") % 2
    totals = jnp.sum(sums[...], axis=0, keepdims=True)
    gram = {}
    for n, (i, j) in enumerate(PAIRS):
        gram[i, j] = gram[j, i] = jnp.broadcast_to(totals[:, n * SUM_LANES : n * SUM_LANES + 1], (1, LANES))

    def inner(left, right):
        return sum(
            left[i] * sum(gram[i, j] * right[j] for j in right) for i in left
        )

    def image(vec):
        out = {}

        def add(at, value):
            out[at] = out[at] + value if at in out else value

        for k, value in vec.items():
            add(k, CENTRE * value)
            if k == 0:
                add(1, RADIUS * value)
            else:
                add(k - 1, RADIUS / 2 * value)
                add(k + 1, RADIUS / 2 * value)
        return out

    one = jnp.ones((1, LANES), F32)
    resid, direction, update = {0: one}, {0: one}, {}
    norm = gram[0, 0]
    for iteration in range(ITERS):
        moved = image(direction)
        step = norm / inner(direction, moved)
        for k, value in direction.items():
            update[k] = update[k] + step * value if k in update else step * value
        resid = {k: (resid[k] if k in resid else 0.0) - step * value for k, value in moved.items()}
        if iteration < ITERS - 1:
            after = inner(resid, resid)
            ratio = after / norm
            direction = {k: value + ratio * direction[k] if k in direction else value for k, value in resid.items()}
            norm = after

    for copy in copies[1:]:
        copy.wait()
    for source, half in ((mine, part), (other, 1 - part)):
        lanes = pl.ds(pl.multiple_of(half * LANES, LANES), LANES)
        for comp in range(2):
            basis = [source[k, comp] for k in range(BASIS)]
            control[comp, :, lanes] = field[comp, :, lanes] + sum(update[k] * basis[k] for k in update)
            residual[comp, :, lanes] = sum(resid[k] * basis[k] for k in resid)


def shards(start_field, seam_target, seam_rows, seam_band, seam_frac, adjacency):
    row_count, col_count = lax.axis_size("row"), lax.axis_size("col")
    axes = ("col", "row")
    vmem = pl.BlockSpec(memory_space=pltpu.VMEM)
    anywhere = pl.BlockSpec(memory_space=pl.ANY)
    small = pltpu.CompilerParams(vmem_limit_bytes=4 * 1024 * 1024)

    def shifted(value, move):
        sources = [(col, row) for col in range(col_count) for row in range(row_count)]
        perm = []
        for col, row in sources:
            to_col, to_row = move(col, row)
            if 0 <= to_col < col_count and 0 <= to_row < row_count:
                perm.append((col * row_count + row, to_col * row_count + to_row))
        return lax.ppermute(value, axes, perm)

    half = jax.ShapeDtypeStruct((HALF_ROWS, SAMPLES), F32)
    own, ahead, back = pl.pallas_call(
        pack_kernel,
        out_shape=(jax.ShapeDtypeStruct((2, HALF_ROWS, SAMPLES), F32), half, half),
        in_specs=[pl.BlockSpec(memory_space=pltpu.SMEM)] + [vmem] * 5,
        out_specs=(vmem, vmem, vmem),
        name="pack",
    )(adjacency, start_field, seam_target, seam_rows, seam_band, seam_frac)

    outward = lambda row: 1 - 2 * (row % 2)
    pieces = (
        own,
        shifted(own, lambda col, row: (col, row ^ 1)),
        shifted(ahead, lambda col, row: (col + outward(row), row)),
        shifted(back, lambda col, row: (col - outward(row), row ^ 1)),
    )
    if row_count > 2:
        from_above = [shifted(piece, lambda col, row: (col, row + 2)) for piece in pieces]
        from_below = [shifted(piece, lambda col, row: (col, row - 2)) for piece in pieces]
        pieces = (*from_above, *pieces, *from_below)
    pairs = len(pieces) // 4
    groups = len(groups_of(pairs)[0])
    limit = pltpu.CompilerParams(vmem_limit_bytes=(groups * 11 // 20 + 8 * pairs + 1) * 1024 * 1024)

    part_shape = jax.ShapeDtypeStruct((BASIS, 2, BLOCK_ROWS, LANES), F32)
    mine, theirs, sums = pl.pallas_call(
        lambda *refs: window_kernel(pairs, *refs),
        out_shape=(part_shape, part_shape, jax.ShapeDtypeStruct((row_count * col_count, LANES), F32)),
        in_specs=[anywhere] * len(pieces),
        out_specs=(vmem, vmem, vmem),
        scratch_shapes=[
            pltpu.VMEM((2 * pairs, PIECES, HALF_ROWS, SAMPLES), F32),
            pltpu.VMEM((BASIS + 1, 2, PIECES, 4 * pairs * GRID + 2 * EDGE, LANES), F32),
            pltpu.VMEM((groups, 2 * LANES, SAMPLES), BF16),
            pltpu.VMEM((groups, 2 * LANES, SAMPLES), BF16),
            pltpu.VMEM((groups, SAMPLES, 2 * LANES), BF16),
            pltpu.VMEM((groups, SAMPLES, 2 * LANES), BF16),
            pltpu.VMEM((groups, 8 * PACK, SAMPLES), F32),
            pltpu.VMEM((groups, 2 * PACK, SAMPLES), F32),
            pltpu.VMEM((groups, 2, 8, LANES), F32),
            pltpu.VMEM((groups, 2, 8, LANES), F32),
            pltpu.VMEM((2, WIDTH, pairs * LANES), F32),
            pltpu.VMEM((2, WIDTH, pairs * LANES), F32),
            pltpu.VMEM((2, PIECES, 4 * pairs, GRID + 2 * EDGE, LANES), F32),
            pltpu.SemaphoreType.DMA((len(pieces),)),
        ],
        compiler_params=limit,
        name="window",
    )(*pieces)

    other = shifted(theirs, lambda col, row: (col, row ^ 1))
    sums = lax.all_to_all(sums, axes, 0, 0, tiled=True)

    out = jax.ShapeDtypeStruct(start_field.shape, F32)
    return pl.pallas_call(
        final_kernel,
        out_shape=(out, out),
        in_specs=[anywhere] * 4,
        out_specs=(vmem, vmem),
        scratch_shapes=[
            pltpu.VMEM(sums.shape, F32),
            pltpu.VMEM(mine.shape, F32),
            pltpu.VMEM(mine.shape, F32),
            pltpu.VMEM(start_field.shape, F32),
            pltpu.SemaphoreType.DMA((4,)),
        ],
        compiler_params=small,
        name="final",
    )(sums, mine, other, start_field)


def solution(mesh):
    placed = (
        P(None, "row", "col"),
        P(None, None, "row", "col"),
        P(None, "row", "col"),
        P(None, "row", "col"),
        P(None, None, "row", "col"),
        P(None, "row", "col"),
    )
    return jax.shard_map(
        shards,
        mesh=mesh,
        in_specs=placed,
        out_specs=(P(None, "row", "col"), P(None, "row", "col")),
        check_vma=False,
    )
```

```python
import jax
import jax.numpy as jnp
from jax import lax
from jax.experimental import pallas as pl
from jax.experimental.pallas import tpu as pltpu
from jax.sharding import PartitionSpec as P

GRID = 32
BAND = 4
ITERS = 3
BEND_WEIGHT = 0.05
DAMPING = 0.5

SAMPLES = 256
LANES = 128
PACK = LANES // GRID
TILE_ROWS = 2
HALF_COLS = 4
PIECES = 3
WINDOW_COLS = PIECES * HALF_COLS
WIDTH = WINDOW_COLS * GRID
BLOCK_ROWS = TILE_ROWS * GRID
MASK_ROWS = 8
TABLE_ROWS = 24
TABLES = BLOCK_ROWS + MASK_ROWS
HALF_ROWS = TABLES + HALF_COLS * TABLE_ROWS
BOUNDS = WINDOW_COLS - 1

LOW, HIGH = 0.5, 6.0
CENTRE, RADIUS = (HIGH + LOW) / 2, (HIGH - LOW) / 2

BASIS = ITERS + 1
PAIRS = [(i, j) for i in range(BASIS) for j in range(i, BASIS)]
SUM_ROWS = 16
SUM_LANES = LANES // SUM_ROWS
EDGE = 8

F32, BF16 = jnp.float32, jnp.bfloat16


def hat(offset):
    return jnp.maximum(1.0 - jnp.abs(offset), 0.0)


def pack_kernel(*refs):
    sources, (own, ahead, back), (*copied, sems) = refs[:6], refs[6:9], refs[9:]
    field, target, rows, band, frac, adjacency = copied
    copies = [
        pltpu.make_async_copy(source, place, sems.at[n]) for n, (source, place) in enumerate(zip(sources, copied))
    ]
    for copy in copies:
        copy.start()
    for copy in copies:
        copy.wait()
    part = lax.axis_index("row") % 2
    not_last_col = (lax.axis_index("col") < lax.axis_size("col") - 1).astype(jnp.int32)
    not_last_row = (lax.axis_index("row") < lax.axis_size("row") - 1).astype(jnp.int32)
    tiles = 2 * HALF_COLS
    sub = lax.broadcasted_iota(jnp.int32, (MASK_ROWS, SAMPLES), 0)
    for half in range(2):
        for comp in range(2):
            own[half, :BLOCK_ROWS, comp * LANES : (comp + 1) * LANES] = field[
                comp, :, half * LANES : (half + 1) * LANES
            ]
    for facing in range(4):
        along = rows[facing].astype(F32) + (frac[facing, 0].astype(F32) + 0.5) / 256.0
        across = band[facing].astype(F32) + (frac[facing, 1].astype(F32) + 0.5) / 256.0
        for tile in range(tiles):
            half, base = tile // HALF_COLS, TABLES + tile % HALF_COLS * TABLE_ROWS + 2 * facing
            lanes = slice(tile * SAMPLES, (tile + 1) * SAMPLES)
            own[half, base : base + 2, :] = along[:, lanes]
            own[half, base + 8 : base + 10, :] = across[:, lanes]
            own[half, base + 16 : base + 18, :] = target[facing // 2, facing % 2][:, lanes]
    place = 2 * sub + lax.broadcasted_iota(jnp.int32, (MASK_ROWS, SAMPLES), 1) // LANES
    for half in range(2):
        masks = jnp.zeros((MASK_ROWS, SAMPLES), F32)
        for tile in range(half * HALF_COLS, (half + 1) * HALF_COLS):
            for side in range(2):
                for row in range(TILE_ROWS):
                    value = adjacency[side, row, tile]
                    if side == 0 and tile == tiles - 1:
                        value = value * not_last_col
                    if side == 1 and row == TILE_ROWS - 1:
                        value = value * not_last_row
                    entry = 4 * (tile % HALF_COLS) + 2 * side + row
                    masks = jnp.where(place == entry, value.astype(F32), masks)
        own[half, BLOCK_ROWS:TABLES, :] = masks
    ahead[...] = own[1 - part]
    back[...] = own[part]


def split(value):
    high = value.astype(BF16)
    return high, (value - high.astype(F32)).astype(BF16)


def groups_of(pairs):
    order, counts = [], []
    for reach in range(ITERS + 1):
        step = ITERS - reach
        for bound in range(step, BOUNDS - step):
            order += [(0, bound, group) for group in range(pairs)]
        for piece in (1,) if step == ITERS else range(PIECES):
            order += [(1, row, piece) for row in range(4 * pairs - 1)]
        order = list(dict.fromkeys(order))
        counts.append(len(order))
    return order, counts[::-1]


def window_kernel(pairs, *refs):
    count = 4 * pairs
    pieces = refs[:count]
    mine, theirs, sums, slots, vecs, weight_hi, weight_lo, turned_hi, turned_lo, cross, shift, *rest = refs[count:]
    strip_in, strip_out, flipped, spread, bends, sems = rest
    order, counts = groups_of(pairs)
    own_pair = pairs // 2
    part = lax.axis_index("row") % 2

    copies = []
    for pair in range(pairs):
        places = (
            slots.at[2 * pair + part, pl.ds(1 - part, 2)],
            slots.at[2 * pair + 1 - part, pl.ds(1 - part, 2)],
            slots.at[2 * pair + part, 2 * part],
            slots.at[2 * pair + 1 - part, 2 * part],
        )
        for kind in range(4):
            at = 4 * pair + kind
            copies.append(pltpu.make_async_copy(pieces[at], places[kind], sems.at[at]))
    for copy in copies:
        copy.start()
    for copy in copies:
        copy.wait()

    sub8 = lax.broadcasted_iota(jnp.int32, (8, LANES), 0)
    lane8 = lax.broadcasted_iota(jnp.int32, (8, LANES), 1)
    near_side = sub8 >= 4
    sub16 = lax.broadcasted_iota(jnp.int32, (16, 2 * LANES), 0)
    lane16 = lax.broadcasted_iota(jnp.int32, (16, 2 * LANES), 1)
    side16 = (lane16 < LANES) == (sub16 % 8 >= 4)
    keep = [
        jnp.where(side16 & (lane16 % LANES // GRID == unit), 1.0, 0.0).astype(BF16)
        for unit in range(PACK)
    ]

    for block in range(2 * pairs):
        for piece in range(PIECES):
            for comp in range(2):
                start = EDGE + block * BLOCK_ROWS
                vecs[0, comp, piece, start : start + BLOCK_ROWS, :] = slots[
                    block, piece, :BLOCK_ROWS, comp * LANES : (comp + 1) * LANES
                ]

    def table(row, col, entry):
        start = TABLES + col % HALF_COLS * TABLE_ROWS + entry
        return slots[row // TILE_ROWS, col // HALF_COLS, start : start + 1, :]

    along_iota = lax.broadcasted_iota(jnp.int32, (GRID, SAMPLES), 0).astype(F32)
    sub_s = lax.broadcasted_iota(jnp.int32, (8, SAMPLES), 0)
    near_s = sub_s >= 4
    depth = jnp.where(near_s, 7 - sub_s, sub_s).astype(F32)

    def set_tables(index, direction, near_tiles, far_tiles):
        hats = []
        for unit in range(PACK):
            both = (near_tiles[unit], far_tiles[unit])
            ys = []
            for side in range(2):
                row, col = both[side]
                entry = 2 * (2 * direction + side) + row % TILE_ROWS
                weight = hat(table(row, col, entry) - along_iota)
                high, low = split(weight)
                start = side * LANES + unit * GRID
                weight_hi[index, start : start + GRID, :] = high
                weight_lo[index, start : start + GRID, :] = low
                hats.append(weight)
                ys.append(table(row, col, 8 + entry))
            row, col = both[0]
            entry = 4 * (col % HALF_COLS) + 2 * direction + row % TILE_ROWS
            at, lane = BLOCK_ROWS + entry // 2, entry % 2 * LANES
            mask = slots[row // TILE_ROWS, col // HALF_COLS, at : at + 1, lane : lane + LANES]
            mask = jnp.concatenate([mask, mask], axis=1)
            signed = jnp.where(near_s, mask, -mask)
            rows = slice(8 * unit, 8 * unit + 8)
            across = hat(jnp.where(near_s, ys[0], ys[1]) - depth) * signed
            cross[index, rows, :] = across
            for comp in range(2):
                shift[index, 2 * unit + comp : 2 * unit + comp + 1, :] = table(
                    row, col, 16 + 4 * direction + 2 * comp + row % TILE_ROWS
                )
        ordered = jnp.concatenate(hats[0::2] + hats[1::2], axis=0).T
        high, low = split(ordered)
        turned_hi[index] = high
        turned_lo[index] = low

    for index, (direction, at, group) in enumerate(order):
        if direction == 0:
            tiles = [(PACK * group + unit, at) for unit in range(PACK)]
            set_tables(index, 0, tiles, [(row, col + 1) for row, col in tiles])
        else:
            tiles = [(at, PACK * group + unit) for unit in range(PACK)]
            set_tables(index, 1, tiles, [(row + 1, col) for row, col in tiles])

    spread[...] = jnp.zeros_like(spread)
    bends[...] = jnp.zeros_like(bends)

    def seam_batch(indices, first):
        half = 8 * 2 * PACK
        gathered = []
        for index in indices:
            high, low = split(jnp.concatenate([strip_in[index, comp] for comp in range(2)], axis=0))
            high = jnp.concatenate([high, high], axis=1)
            low = jnp.concatenate([low, low], axis=1)
            left = jnp.concatenate([high * keep[unit] for unit in range(PACK)] + [low * keep[unit] for unit in range(PACK)], axis=0)
            both = jnp.dot(left, weight_hi[index], preferred_element_type=F32)
            rest = jnp.dot(left[:half], weight_lo[index], preferred_element_type=F32)
            gathered.append(both[:half] + both[half:] + rest)
        pulled = []
        for index, values in zip(indices, gathered):
            parts = []
            for unit in range(PACK):
                across = cross[index, 8 * unit : 8 * unit + 8, :]
                for comp in range(2):
                    at = 2 * unit + comp
                    total = jnp.sum(values[8 * at : 8 * at + 8] * across, axis=0, keepdims=True)
                    if first:
                        total = total - shift[index, at : at + 1, :]
                    parts.append(total * across)
            pulled.append(split(jnp.concatenate(parts, axis=0)))
        numbers = (((1,), (0,)), ((), ()))
        backs = []
        for index, (high, low) in zip(indices, pulled):
            both = lax.dot_general(
                jnp.concatenate([high, low], axis=0), turned_hi[index], numbers, preferred_element_type=F32
            )
            rest = lax.dot_general(high, turned_lo[index], numbers, preferred_element_type=F32)
            backs.append(both[:half] + both[half:] + rest)
        for index, back in zip(indices, backs):
            for comp in range(2):
                out = None
                for unit in range(PACK):
                    at = 8 * (2 * unit + comp)
                    chosen = jnp.where(near_side, back[at : at + 8, :LANES], back[at : at + 8, LANES:])
                    out = chosen if out is None else jnp.where(lane8 // GRID == unit, chosen, out)
                strip_out[index, comp] = out

    sub32 = lax.broadcasted_iota(jnp.int32, (GRID, LANES), 0)
    lane32 = lax.broadcasted_iota(jnp.int32, (GRID, LANES), 1) % GRID
    inner = (sub32 >= 1) & (sub32 <= GRID - 2) & (lane32 >= 1) & (lane32 <= GRID - 2)

    def beside(value):
        return pltpu.roll(value, 1, 1) + pltpu.roll(value, LANES - 1, 1) - 4.0 * value

    def apply(step, scale, own_weight, last_weight):
        for comp in range(2):
            for group in range(pairs):
                for piece in range(PIECES):
                    start = EDGE + group * LANES
                    flipped[comp, piece * LANES : (piece + 1) * LANES, group * LANES : (group + 1) * LANES] = vecs[
                        step, comp, piece, start : start + LANES, :
                    ].T
        used = order[: counts[step]]

        def place(entry):
            direction, at, group = entry
            return GRID * at + GRID - 8, group, slice(group * LANES, (group + 1) * LANES), direction == 0

        for index, entry in enumerate(used):
            at, piece, lanes, east = place(entry)
            for comp in range(2):
                if east:
                    before, after = flipped[comp, at : at + 8, lanes], flipped[comp, at + 8 : at + 16, lanes]
                else:
                    start = EDGE + at
                    before = vecs[step, comp, piece, start : start + 8, :]
                    after = vecs[step, comp, piece, start + 8 : start + 16, :]
                strip_in[index, comp] = jnp.where(near_side, before, after)

        seam_batch(list(range(len(used))), step == 0)

        for index, entry in enumerate(used):
            at, piece, lanes, east = place(entry)
            if east:
                for comp in range(2):
                    spread[comp, at : at + 8, lanes] = jnp.where(near_side, strip_out[index, comp], 0.0)
                    spread[comp, at + 8 : at + 16, lanes] = jnp.where(near_side, 0.0, strip_out[index, comp])
        for piece in (1,) if step == ITERS else range(PIECES):
            for comp in range(2):
                for group in range(pairs):
                    turned = spread[
                        comp, piece * LANES : (piece + 1) * LANES, group * LANES : (group + 1) * LANES
                    ].T
                    for unit in range(PACK):
                        tile = PACK * group + unit
                        start = EDGE + tile * GRID
                        value = vecs[step, comp, piece, start : start + GRID, :]
                        level = jnp.where(
                            inner,
                            vecs[step, comp, piece, start - 1 : start + GRID - 1, :]
                            + vecs[step, comp, piece, start + 1 : start + GRID + 1, :]
                            + beside(value),
                            0.0,
                        )
                        bends[comp, piece, tile, EDGE : EDGE + GRID, :] = level
                        curved = (
                            bends[comp, piece, tile, EDGE - 1 : EDGE + GRID - 1, :]
                            + bends[comp, piece, tile, EDGE + 1 : EDGE + GRID + 1, :]
                            + beside(level)
                        )
                        out = scale * (turned[unit * GRID : (unit + 1) * GRID] + BEND_WEIGHT * curved)
                        if own_weight:
                            out = out + own_weight * value
                        if last_weight:
                            out = out + last_weight * vecs[step - 1, comp, piece, start : start + GRID, :]
                        vecs[step + 1, comp, piece, start : start + GRID, :] = out
        for index, entry in enumerate(used):
            at, piece, lanes, east = place(entry)
            if not east:
                start = EDGE + at
                for comp in range(2):
                    result = scale * strip_out[index, comp]
                    vecs[step + 1, comp, piece, start : start + 8, :] += jnp.where(near_side, result, 0.0)
                    vecs[step + 1, comp, piece, start + 8 : start + 16, :] += jnp.where(near_side, 0.0, result)

    apply(0, -1.0, 0.0, 0.0)
    apply(1, 1.0 / RADIUS, (DAMPING - CENTRE) / RADIUS, 0.0)
    apply(2, 2.0 / RADIUS, 2.0 * (DAMPING - CENTRE) / RADIUS, -1.0)
    apply(3, 2.0 / RADIUS, 2.0 * (DAMPING - CENTRE) / RADIUS, -1.0)

    first_row = EDGE + own_pair * 2 * BLOCK_ROWS
    partial = [jnp.zeros((8, LANES), F32) for _ in PAIRS]
    for comp in range(2):
        for row in range(first_row, first_row + 2 * BLOCK_ROWS, 8):
            values = [vecs[1 + k, comp, 1, row : row + 8, :] for k in range(BASIS)]
            for n, (i, j) in enumerate(PAIRS):
                partial[n] = partial[n] + values[i] * values[j]
    rows = [jnp.sum(value, axis=0, keepdims=True) for value in partial]
    rows.append(jnp.zeros((SUM_ROWS - len(rows), LANES), F32))
    totals = jnp.sum(jnp.concatenate(rows, axis=0), axis=1, keepdims=True)
    slot = lax.broadcasted_iota(jnp.int32, (SUM_ROWS, LANES), 1) // SUM_LANES
    placed = jnp.where(slot == lax.broadcasted_iota(jnp.int32, (SUM_ROWS, LANES), 0), totals, 0.0)
    sums[...] = jnp.broadcast_to(jnp.sum(placed, axis=0, keepdims=True), sums.shape)
    for k in range(BASIS):
        for comp in range(2):
            for out, block in ((mine, part), (theirs, 1 - part)):
                start = pl.multiple_of(first_row + block * BLOCK_ROWS, EDGE)
                out[k, comp] = vecs[1 + k, comp, 1, pl.ds(start, BLOCK_ROWS), :]


def final_kernel(*refs):
    sources, (control, residual), (sums, mine, other, field, sems) = refs[:4], refs[4:6], refs[6:]
    copies = [
        pltpu.make_async_copy(source, target, sems.at[n])
        for n, (source, target) in enumerate(zip(sources, (sums, mine, other, field)))
    ]
    for copy in copies:
        copy.start()
    copies[0].wait()
    part = lax.axis_index("row") % 2
    totals = jnp.sum(sums[...], axis=0, keepdims=True)
    gram = {}
    for n, (i, j) in enumerate(PAIRS):
        gram[i, j] = gram[j, i] = jnp.broadcast_to(totals[:, n * SUM_LANES : n * SUM_LANES + 1], (1, LANES))

    def inner(left, right):
        return sum(
            left[i] * sum(gram[i, j] * right[j] for j in right) for i in left
        )

    def image(vec):
        out = {}

        def add(at, value):
            out[at] = out[at] + value if at in out else value

        for k, value in vec.items():
            add(k, CENTRE * value)
            if k == 0:
                add(1, RADIUS * value)
            else:
                add(k - 1, RADIUS / 2 * value)
                add(k + 1, RADIUS / 2 * value)
        return out

    one = jnp.ones((1, LANES), F32)
    resid, direction, update = {0: one}, {0: one}, {}
    norm = gram[0, 0]
    for iteration in range(ITERS):
        moved = image(direction)
        step = norm / inner(direction, moved)
        for k, value in direction.items():
            update[k] = update[k] + step * value if k in update else step * value
        resid = {k: (resid[k] if k in resid else 0.0) - step * value for k, value in moved.items()}
        if iteration < ITERS - 1:
            after = inner(resid, resid)
            ratio = after / norm
            direction = {k: value + ratio * direction[k] if k in direction else value for k, value in resid.items()}
            norm = after

    for copy in copies[1:]:
        copy.wait()
    for source, half in ((mine, part), (other, 1 - part)):
        lanes = pl.ds(pl.multiple_of(half * LANES, LANES), LANES)
        for comp in range(2):
            basis = [source[k, comp] for k in range(BASIS)]
            control[comp, :, lanes] = field[comp, :, lanes] + sum(update[k] * basis[k] for k in update)
            residual[comp, :, lanes] = sum(resid[k] * basis[k] for k in resid)


def shards(start_field, seam_target, seam_rows, seam_band, seam_frac, adjacency):
    row_count, col_count = lax.axis_size("row"), lax.axis_size("col")
    axes = ("col", "row")
    vmem = pl.BlockSpec(memory_space=pltpu.VMEM)
    anywhere = pl.BlockSpec(memory_space=pl.ANY)
    small = pltpu.CompilerParams(vmem_limit_bytes=4 * 1024 * 1024)

    def shifted(value, move):
        sources = [(col, row) for col in range(col_count) for row in range(row_count)]
        perm = []
        for col, row in sources:
            to_col, to_row = move(col, row)
            if 0 <= to_col < col_count and 0 <= to_row < row_count:
                perm.append((col * row_count + row, to_col * row_count + to_row))
        return lax.ppermute(value, axes, perm)

    half = jax.ShapeDtypeStruct((HALF_ROWS, SAMPLES), F32)
    inputs = (start_field, seam_target, seam_rows, seam_band, seam_frac, adjacency)
    own, ahead, back = pl.pallas_call(
        pack_kernel,
        out_shape=(jax.ShapeDtypeStruct((2, HALF_ROWS, SAMPLES), F32), half, half),
        in_specs=[anywhere] * 6,
        out_specs=(vmem, vmem, vmem),
        scratch_shapes=[pltpu.VMEM(value.shape, value.dtype) for value in inputs[:5]]
        + [pltpu.SMEM(adjacency.shape, adjacency.dtype), pltpu.SemaphoreType.DMA((6,))],
        compiler_params=small,
        name="pack",
    )(*(pltpu.with_memory_space_constraint(value, pltpu.HBM) for value in inputs))

    outward = lambda row: 1 - 2 * (row % 2)
    pieces = (
        own,
        shifted(own, lambda col, row: (col, row ^ 1)),
        shifted(ahead, lambda col, row: (col + outward(row), row)),
        shifted(back, lambda col, row: (col - outward(row), row ^ 1)),
    )
    if row_count > 2:
        from_above = [shifted(piece, lambda col, row: (col, row + 2)) for piece in pieces]
        from_below = [shifted(piece, lambda col, row: (col, row - 2)) for piece in pieces]
        pieces = (*from_above, *pieces, *from_below)
    pairs = len(pieces) // 4
    groups = len(groups_of(pairs)[0])
    limit = pltpu.CompilerParams(vmem_limit_bytes=(groups * 11 // 20 + 8 * pairs + 1) * 1024 * 1024)

    part_shape = jax.ShapeDtypeStruct((BASIS, 2, BLOCK_ROWS, LANES), F32)
    mine, theirs, sums = pl.pallas_call(
        lambda *refs: window_kernel(pairs, *refs),
        out_shape=(part_shape, part_shape, jax.ShapeDtypeStruct((row_count * col_count, LANES), F32)),
        in_specs=[anywhere] * len(pieces),
        out_specs=(vmem, vmem, vmem),
        scratch_shapes=[
            pltpu.VMEM((2 * pairs, PIECES, HALF_ROWS, SAMPLES), F32),
            pltpu.VMEM((BASIS + 1, 2, PIECES, 4 * pairs * GRID + 2 * EDGE, LANES), F32),
            pltpu.VMEM((groups, 2 * LANES, SAMPLES), BF16),
            pltpu.VMEM((groups, 2 * LANES, SAMPLES), BF16),
            pltpu.VMEM((groups, SAMPLES, 2 * LANES), BF16),
            pltpu.VMEM((groups, SAMPLES, 2 * LANES), BF16),
            pltpu.VMEM((groups, 8 * PACK, SAMPLES), F32),
            pltpu.VMEM((groups, 2 * PACK, SAMPLES), F32),
            pltpu.VMEM((groups, 2, 8, LANES), F32),
            pltpu.VMEM((groups, 2, 8, LANES), F32),
            pltpu.VMEM((2, WIDTH, pairs * LANES), F32),
            pltpu.VMEM((2, WIDTH, pairs * LANES), F32),
            pltpu.VMEM((2, PIECES, 4 * pairs, GRID + 2 * EDGE, LANES), F32),
            pltpu.SemaphoreType.DMA((len(pieces),)),
        ],
        compiler_params=limit,
        name="window",
    )(*pieces)

    other = shifted(theirs, lambda col, row: (col, row ^ 1))
    sums = lax.all_to_all(sums, axes, 0, 0, tiled=True)

    out = jax.ShapeDtypeStruct(start_field.shape, F32)
    return pl.pallas_call(
        final_kernel,
        out_shape=(out, out),
        in_specs=[anywhere] * 4,
        out_specs=(vmem, vmem),
        scratch_shapes=[
            pltpu.VMEM(sums.shape, F32),
            pltpu.VMEM(mine.shape, F32),
            pltpu.VMEM(mine.shape, F32),
            pltpu.VMEM(start_field.shape, F32),
            pltpu.SemaphoreType.DMA((4,)),
        ],
        compiler_params=small,
        name="final",
    )(sums, mine, other, start_field)


def solution(mesh):
    placed = (
        P(None, "row", "col"),
        P(None, None, "row", "col"),
        P(None, "row", "col"),
        P(None, "row", "col"),
        P(None, None, "row", "col"),
        P(None, "row", "col"),
    )
    return jax.shard_map(
        shards,
        mesh=mesh,
        in_specs=placed,
        out_specs=(P(None, "row", "col"), P(None, "row", "col")),
        check_vma=False,
    )
```

```python
import jax
import jax.numpy as jnp
from jax import lax
from jax.experimental import pallas as pl
from jax.experimental.pallas import tpu as pltpu
from jax.sharding import PartitionSpec as P

GRID = 32
BAND = 4
ITERS = 3
BEND_WEIGHT = 0.05
DAMPING = 0.5

SAMPLES = 256
LANES = 128
PACK = LANES // GRID
TILE_ROWS = 2
HALF_COLS = 4
PIECES = 3
WINDOW_COLS = PIECES * HALF_COLS
WIDTH = WINDOW_COLS * GRID
BLOCK_ROWS = TILE_ROWS * GRID
MASK_ROWS = 8
TABLE_ROWS = 24
TABLES = BLOCK_ROWS + MASK_ROWS
HALF_ROWS = TABLES + HALF_COLS * TABLE_ROWS
BOUNDS = WINDOW_COLS - 1
PLACED = ((0, 1, 10, 11), (4, 5, 6, 7), (8, 9, 2, 3))

LOW, HIGH = 0.5, 6.0
CENTRE, RADIUS = (HIGH + LOW) / 2, (HIGH - LOW) / 2

BASIS = ITERS + 1
PAIRS = [(i, j) for i in range(BASIS) for j in range(i, BASIS)]
SUM_ROWS = 16
SUM_LANES = LANES // SUM_ROWS
EDGE = 8

F32, BF16 = jnp.float32, jnp.bfloat16


def hat(offset):
    return jnp.maximum(1.0 - jnp.abs(offset), 0.0)


def pack_kernel(*refs):
    sources, (own, ahead, back), (*copied, sems) = refs[:6], refs[6:9], refs[9:]
    field, target, rows, band, frac, adjacency = copied
    copies = [
        pltpu.make_async_copy(source, place, sems.at[n]) for n, (source, place) in enumerate(zip(sources, copied))
    ]
    for copy in copies:
        copy.start()
    for copy in copies:
        copy.wait()
    part = lax.axis_index("row") % 2
    not_last_col = (lax.axis_index("col") < lax.axis_size("col") - 1).astype(jnp.int32)
    not_last_row = (lax.axis_index("row") < lax.axis_size("row") - 1).astype(jnp.int32)
    tiles = 2 * HALF_COLS
    sub = lax.broadcasted_iota(jnp.int32, (MASK_ROWS, SAMPLES), 0)
    for half in range(2):
        for comp in range(2):
            own[half, :BLOCK_ROWS, comp * LANES : (comp + 1) * LANES] = field[
                comp, :, half * LANES : (half + 1) * LANES
            ]
    for facing in range(4):
        along = rows[facing].astype(F32) + (frac[facing, 0].astype(F32) + 0.5) / 256.0
        across = band[facing].astype(F32) + (frac[facing, 1].astype(F32) + 0.5) / 256.0
        for tile in range(tiles):
            half, base = tile // HALF_COLS, TABLES + tile % HALF_COLS * TABLE_ROWS + 2 * facing
            lanes = slice(tile * SAMPLES, (tile + 1) * SAMPLES)
            own[half, base : base + 2, :] = along[:, lanes]
            own[half, base + 8 : base + 10, :] = across[:, lanes]
            own[half, base + 16 : base + 18, :] = target[facing // 2, facing % 2][:, lanes]
    place = 2 * sub + lax.broadcasted_iota(jnp.int32, (MASK_ROWS, SAMPLES), 1) // LANES
    for half in range(2):
        masks = jnp.zeros((MASK_ROWS, SAMPLES), F32)
        for tile in range(half * HALF_COLS, (half + 1) * HALF_COLS):
            for side in range(2):
                for row in range(TILE_ROWS):
                    value = adjacency[side, row, tile]
                    if side == 0 and tile == tiles - 1:
                        value = value * not_last_col
                    if side == 1 and row == TILE_ROWS - 1:
                        value = value * not_last_row
                    entry = 4 * (tile % HALF_COLS) + 2 * side + row
                    masks = jnp.where(place == entry, value.astype(F32), masks)
        own[half, BLOCK_ROWS:TABLES, :] = masks
    ahead[...] = own[1 - part]
    back[...] = own[part]


def split(value):
    high = value.astype(BF16)
    return high, (value - high.astype(F32)).astype(BF16)


def position(col):
    for piece, cols in enumerate(PLACED):
        if col in cols:
            return piece * LANES + cols.index(col) * GRID


def pieces_at(step):
    return ((1, 2, 0), (1, 2), (1, 2), (1,))[step]


def groups_of(pairs):
    order, counts = [], []
    for reach in range(ITERS + 1):
        step = ITERS - reach
        for bound in range(step, BOUNDS - step):
            order += [(0, bound, group) for group in range(pairs)]
        for piece in pieces_at(step):
            order += [(1, row, piece) for row in range(4 * pairs - 1)]
        order = list(dict.fromkeys(order))
        counts.append(len(order))
    return order, counts[::-1]


def window_kernel(pairs, *refs):
    count = 4 * pairs
    pieces = refs[:count]
    mine, theirs, sums, slots, vecs, weight_hi, weight_lo, turned_hi, turned_lo, cross, shift, *rest = refs[count:]
    flipped, spread, bends, sems = rest
    order, counts = groups_of(pairs)
    own_pair = pairs // 2
    part = lax.axis_index("row") % 2

    copies = []
    for pair in range(pairs):
        places = (
            slots.at[2 * pair + part, pl.ds(1 - part, 2)],
            slots.at[2 * pair + 1 - part, pl.ds(1 - part, 2)],
            slots.at[2 * pair + part, 2 * part],
            slots.at[2 * pair + 1 - part, 2 * part],
        )
        for kind in range(4):
            at = 4 * pair + kind
            copies.append(pltpu.make_async_copy(pieces[at], places[kind], sems.at[at]))
    for copy in copies:
        copy.start()
    for copy in copies:
        copy.wait()

    sub8 = lax.broadcasted_iota(jnp.int32, (8, LANES), 0)
    lane8 = lax.broadcasted_iota(jnp.int32, (8, LANES), 1)
    near_side = sub8 >= 4
    sub16 = lax.broadcasted_iota(jnp.int32, (16, 2 * LANES), 0)
    lane16 = lax.broadcasted_iota(jnp.int32, (16, 2 * LANES), 1)
    side16 = (lane16 < LANES) == (sub16 % 8 >= 4)
    keep = [
        jnp.where(side16 & (lane16 % LANES // GRID == unit), 1.0, 0.0).astype(BF16)
        for unit in range(PACK)
    ]

    low_lanes = lax.broadcasted_iota(jnp.int32, (BLOCK_ROWS, LANES), 1) < LANES // 2
    for block in range(2 * pairs):
        start = EDGE + block * BLOCK_ROWS
        for comp in range(2):
            left, middle, right = (
                slots[block, piece, :BLOCK_ROWS, comp * LANES : (comp + 1) * LANES] for piece in range(PIECES)
            )
            placed = (jnp.where(low_lanes, left, right), middle, jnp.where(low_lanes, right, left))
            for piece in range(PIECES):
                vecs[0, comp, piece, start : start + BLOCK_ROWS, :] = placed[piece]

    def table(row, col, entry):
        start = TABLES + col % HALF_COLS * TABLE_ROWS + entry
        return slots[row // TILE_ROWS, col // HALF_COLS, start : start + 1, :]

    along_iota = lax.broadcasted_iota(jnp.int32, (GRID, SAMPLES), 0).astype(F32)
    sub_s = lax.broadcasted_iota(jnp.int32, (8, SAMPLES), 0)
    near_s = sub_s >= 4
    depth = jnp.where(near_s, 7 - sub_s, sub_s).astype(F32)

    def set_tables(index, direction, near_tiles, far_tiles):
        hats = []
        for unit in range(PACK):
            both = (near_tiles[unit], far_tiles[unit])
            ys = []
            for side in range(2):
                row, col = both[side]
                entry = 2 * (2 * direction + side) + row % TILE_ROWS
                weight = hat(table(row, col, entry) - along_iota)
                high, low = split(weight)
                start = side * LANES + unit * GRID
                weight_hi[index, start : start + GRID, :] = high
                weight_lo[index, start : start + GRID, :] = low
                hats.append(weight)
                ys.append(table(row, col, 8 + entry))
            row, col = both[0]
            entry = 4 * (col % HALF_COLS) + 2 * direction + row % TILE_ROWS
            at, lane = BLOCK_ROWS + entry // 2, entry % 2 * LANES
            mask = slots[row // TILE_ROWS, col // HALF_COLS, at : at + 1, lane : lane + LANES]
            mask = jnp.concatenate([mask, mask], axis=1)
            signed = jnp.where(near_s, mask, -mask)
            rows = slice(8 * unit, 8 * unit + 8)
            across = hat(jnp.where(near_s, ys[0], ys[1]) - depth) * signed
            cross[index, rows, :] = across
            for comp in range(2):
                shift[index, 2 * unit + comp : 2 * unit + comp + 1, :] = table(
                    row, col, 16 + 4 * direction + 2 * comp + row % TILE_ROWS
                )
        ordered = jnp.concatenate(hats[0::2] + hats[1::2], axis=0).T
        high, low = split(ordered)
        turned_hi[index] = high
        turned_lo[index] = low

    for index, (direction, at, group) in enumerate(order):
        if direction == 0:
            tiles = [(PACK * group + unit, at) for unit in range(PACK)]
            set_tables(index, 0, tiles, [(row, col + 1) for row, col in tiles])
        else:
            tiles = [(at, col) for col in PLACED[group]]
            set_tables(index, 1, tiles, [(row + 1, col) for row, col in tiles])

    spread[...] = jnp.zeros_like(spread)
    bends[...] = jnp.zeros_like(bends)

    def seam_group(index, strips, first):
        half = 8 * 2 * PACK
        high, low = split(jnp.concatenate(strips, axis=0))
        high = jnp.concatenate([high, high], axis=1)
        low = jnp.concatenate([low, low], axis=1)
        left = jnp.concatenate([part * keep[unit] for part in (high, low) for unit in range(PACK)], axis=0)
        both = jnp.dot(left, weight_hi[index], preferred_element_type=F32)
        values = both[:half] + both[half:] + jnp.dot(left[:half], weight_lo[index], preferred_element_type=F32)
        pulled = []
        for unit in range(PACK):
            across = cross[index, 8 * unit : 8 * unit + 8, :]
            for comp in range(2):
                at = 2 * unit + comp
                total = jnp.sum(values[8 * at : 8 * at + 8] * across, axis=0, keepdims=True)
                if first:
                    total = total - shift[index, at : at + 1, :]
                pulled.append(total * across)
        high, low = split(jnp.concatenate(pulled, axis=0))
        both = jnp.dot(jnp.concatenate([high, low], axis=0), turned_hi[index], preferred_element_type=F32)
        back = both[:half] + both[half:] + jnp.dot(high, turned_lo[index], preferred_element_type=F32)
        results = []
        for comp in range(2):
            out = None
            for unit in range(PACK):
                at = 8 * (2 * unit + comp)
                chosen = jnp.where(near_side, back[at : at + 8, :LANES], back[at : at + 8, LANES:])
                out = chosen if out is None else jnp.where(lane8 // GRID == unit, chosen, out)
            results.append(out)
        return results

    sub32 = lax.broadcasted_iota(jnp.int32, (GRID, LANES), 0)
    lane32 = lax.broadcasted_iota(jnp.int32, (GRID, LANES), 1) % GRID
    inner = (sub32 >= 1) & (sub32 <= GRID - 2) & (lane32 >= 1) & (lane32 <= GRID - 2)

    def beside(value):
        return pltpu.roll(value, 1, 1) + pltpu.roll(value, LANES - 1, 1) - 4.0 * value

    def apply(step, scale, own_weight, last_weight):
        for comp in range(2):
            for group in range(pairs):
                for piece in range(PIECES) if step < 2 else (1, 2):
                    start = EDGE + group * LANES
                    flipped[comp, piece * LANES : (piece + 1) * LANES, group * LANES : (group + 1) * LANES] = vecs[
                        step, comp, piece, start : start + LANES, :
                    ].T
        used = order[: counts[step]]

        def place(entry):
            direction, at, group = entry
            lanes = slice(group * LANES, (group + 1) * LANES)
            if direction == 0:
                return True, position(at) + GRID - 8, position(at + 1), lanes
            return False, EDGE + GRID * at + GRID - 8, EDGE + GRID * (at + 1), group

        def take_strips(entry):
            east, before, after, where = place(entry)
            strips = []
            for comp in range(2):
                source = flipped.at[comp, :, where] if east else vecs.at[step, comp, where]
                strips.append(jnp.where(near_side, source[before : before + 8, :], source[after : after + 8, :]))
            return strips

        for index, entry in enumerate(used):
            east, before, after, where = place(entry)
            if east:
                results = seam_group(index, take_strips(entry), step == 0)
                for comp in range(2):
                    result = scale * results[comp]
                    spread[comp, before : before + 8, where] = jnp.where(near_side, result, 0.0)
                    spread[comp, after : after + 8, where] = jnp.where(near_side, 0.0, result)
        for piece in pieces_at(step):
            for comp in range(2):
                for tile in range(4 * pairs):
                    start = EDGE + tile * GRID
                    value = vecs[step, comp, piece, start : start + GRID, :]
                    level = jnp.where(
                        inner,
                        vecs[step, comp, piece, start - 1 : start + GRID - 1, :]
                        + vecs[step, comp, piece, start + 1 : start + GRID + 1, :]
                        + beside(value),
                        0.0,
                    )
                    bends[comp, piece, tile, EDGE : EDGE + GRID, :] = level
                    out = (scale * BEND_WEIGHT) * (
                        bends[comp, piece, tile, EDGE - 1 : EDGE + GRID - 1, :]
                        + bends[comp, piece, tile, EDGE + 1 : EDGE + GRID + 1, :]
                        + beside(level)
                    )
                    if own_weight:
                        out = out + own_weight * value
                    if last_weight:
                        out = out + last_weight * vecs[step - 1, comp, piece, start : start + GRID, :]
                    vecs[step + 1, comp, piece, start : start + GRID, :] = out
        for index, entry in enumerate(used):
            east, before, after, where = place(entry)
            if not east:
                results = seam_group(index, take_strips(entry), step == 0)
                for comp in range(2):
                    result = scale * results[comp]
                    vecs[step + 1, comp, where, before : before + 8, :] += jnp.where(near_side, result, 0.0)
                    vecs[step + 1, comp, where, after : after + 8, :] += jnp.where(near_side, 0.0, result)
        for piece in pieces_at(step):
            for comp in range(2):
                for group in range(pairs):
                    start = EDGE + group * LANES
                    vecs[step + 1, comp, piece, start : start + LANES, :] += spread[
                        comp, piece * LANES : (piece + 1) * LANES, group * LANES : (group + 1) * LANES
                    ].T

    apply(0, -1.0, 0.0, 0.0)
    apply(1, 1.0 / RADIUS, (DAMPING - CENTRE) / RADIUS, 0.0)
    apply(2, 2.0 / RADIUS, 2.0 * (DAMPING - CENTRE) / RADIUS, -1.0)
    apply(3, 2.0 / RADIUS, 2.0 * (DAMPING - CENTRE) / RADIUS, -1.0)

    first_row = EDGE + own_pair * 2 * BLOCK_ROWS
    partial = [jnp.zeros((8, LANES), F32) for _ in PAIRS]
    for comp in range(2):
        for row in range(first_row, first_row + 2 * BLOCK_ROWS, 8):
            values = [vecs[1 + k, comp, 1, row : row + 8, :] for k in range(BASIS)]
            for n, (i, j) in enumerate(PAIRS):
                partial[n] = partial[n] + values[i] * values[j]
    rows = [jnp.sum(value, axis=0, keepdims=True) for value in partial]
    rows.append(jnp.zeros((SUM_ROWS - len(rows), LANES), F32))
    totals = jnp.sum(jnp.concatenate(rows, axis=0), axis=1, keepdims=True)
    slot = lax.broadcasted_iota(jnp.int32, (SUM_ROWS, LANES), 1) // SUM_LANES
    placed = jnp.where(slot == lax.broadcasted_iota(jnp.int32, (SUM_ROWS, LANES), 0), totals, 0.0)
    sums[...] = jnp.broadcast_to(jnp.sum(placed, axis=0, keepdims=True), sums.shape)
    for k in range(BASIS):
        for comp in range(2):
            for out, block in ((mine, part), (theirs, 1 - part)):
                start = pl.multiple_of(first_row + block * BLOCK_ROWS, EDGE)
                out[k, comp] = vecs[1 + k, comp, 1, pl.ds(start, BLOCK_ROWS), :]


def final_kernel(*refs):
    sources, (control, residual), (sums, mine, other, field, sems) = refs[:4], refs[4:6], refs[6:]
    copies = [
        pltpu.make_async_copy(source, target, sems.at[n])
        for n, (source, target) in enumerate(zip(sources, (sums, mine, other, field)))
    ]
    for copy in copies:
        copy.start()
    copies[0].wait()
    part = lax.axis_index("row") % 2
    totals = jnp.sum(sums[...], axis=0, keepdims=True)
    gram = {}
    for n, (i, j) in enumerate(PAIRS):
        gram[i, j] = gram[j, i] = jnp.broadcast_to(totals[:, n * SUM_LANES : n * SUM_LANES + 1], (1, LANES))

    def inner(left, right):
        return sum(
            left[i] * sum(gram[i, j] * right[j] for j in right) for i in left
        )

    def image(vec):
        out = {}

        def add(at, value):
            out[at] = out[at] + value if at in out else value

        for k, value in vec.items():
            add(k, CENTRE * value)
            if k == 0:
                add(1, RADIUS * value)
            else:
                add(k - 1, RADIUS / 2 * value)
                add(k + 1, RADIUS / 2 * value)
        return out

    one = jnp.ones((1, LANES), F32)
    resid, direction, update = {0: one}, {0: one}, {}
    norm = gram[0, 0]
    for iteration in range(ITERS):
        moved = image(direction)
        step = norm / inner(direction, moved)
        for k, value in direction.items():
            update[k] = update[k] + step * value if k in update else step * value
        resid = {k: (resid[k] if k in resid else 0.0) - step * value for k, value in moved.items()}
        if iteration < ITERS - 1:
            after = inner(resid, resid)
            ratio = after / norm
            direction = {k: value + ratio * direction[k] if k in direction else value for k, value in resid.items()}
            norm = after

    for copy in copies[1:]:
        copy.wait()
    for source, half in ((mine, part), (other, 1 - part)):
        lanes = pl.ds(pl.multiple_of(half * LANES, LANES), LANES)
        for comp in range(2):
            basis = [source[k, comp] for k in range(BASIS)]
            control[comp, :, lanes] = field[comp, :, lanes] + sum(update[k] * basis[k] for k in update)
            residual[comp, :, lanes] = sum(resid[k] * basis[k] for k in resid)


def shards(start_field, seam_target, seam_rows, seam_band, seam_frac, adjacency):
    row_count, col_count = lax.axis_size("row"), lax.axis_size("col")
    axes = ("col", "row")
    vmem = pl.BlockSpec(memory_space=pltpu.VMEM)
    anywhere = pl.BlockSpec(memory_space=pl.ANY)
    small = pltpu.CompilerParams(vmem_limit_bytes=4 * 1024 * 1024)

    def shifted(value, move):
        sources = [(col, row) for col in range(col_count) for row in range(row_count)]
        perm = []
        for col, row in sources:
            to_col, to_row = move(col, row)
            if 0 <= to_col < col_count and 0 <= to_row < row_count:
                perm.append((col * row_count + row, to_col * row_count + to_row))
        return lax.ppermute(value, axes, perm)

    half = jax.ShapeDtypeStruct((HALF_ROWS, SAMPLES), F32)
    inputs = (start_field, seam_target, seam_rows, seam_band, seam_frac, adjacency)
    own, ahead, back = pl.pallas_call(
        pack_kernel,
        out_shape=(jax.ShapeDtypeStruct((2, HALF_ROWS, SAMPLES), F32), half, half),
        in_specs=[anywhere] * 6,
        out_specs=(vmem, vmem, vmem),
        scratch_shapes=[pltpu.VMEM(value.shape, value.dtype) for value in inputs[:5]]
        + [pltpu.SMEM(adjacency.shape, adjacency.dtype), pltpu.SemaphoreType.DMA((6,))],
        compiler_params=small,
        name="pack",
    )(*(pltpu.with_memory_space_constraint(value, pltpu.HBM) for value in inputs))

    outward = lambda row: 1 - 2 * (row % 2)
    pieces = (
        own,
        shifted(own, lambda col, row: (col, row ^ 1)),
        shifted(ahead, lambda col, row: (col + outward(row), row)),
        shifted(back, lambda col, row: (col - outward(row), row ^ 1)),
    )
    if row_count > 2:
        from_above = [shifted(piece, lambda col, row: (col, row + 2)) for piece in pieces]
        from_below = [shifted(piece, lambda col, row: (col, row - 2)) for piece in pieces]
        pieces = (*from_above, *pieces, *from_below)
    pairs = len(pieces) // 4
    groups = len(groups_of(pairs)[0])
    limit = pltpu.CompilerParams(vmem_limit_bytes=(groups * 11 // 20 + 8 * pairs + 1) * 1024 * 1024)

    part_shape = jax.ShapeDtypeStruct((BASIS, 2, BLOCK_ROWS, LANES), F32)
    mine, theirs, sums = pl.pallas_call(
        lambda *refs: window_kernel(pairs, *refs),
        out_shape=(part_shape, part_shape, jax.ShapeDtypeStruct((row_count * col_count, LANES), F32)),
        in_specs=[anywhere] * len(pieces),
        out_specs=(vmem, vmem, vmem),
        scratch_shapes=[
            pltpu.VMEM((2 * pairs, PIECES, HALF_ROWS, SAMPLES), F32),
            pltpu.VMEM((BASIS + 1, 2, PIECES, 4 * pairs * GRID + 2 * EDGE, LANES), F32),
            pltpu.VMEM((groups, 2 * LANES, SAMPLES), BF16),
            pltpu.VMEM((groups, 2 * LANES, SAMPLES), BF16),
            pltpu.VMEM((groups, SAMPLES, 2 * LANES), BF16),
            pltpu.VMEM((groups, SAMPLES, 2 * LANES), BF16),
            pltpu.VMEM((groups, 8 * PACK, SAMPLES), F32),
            pltpu.VMEM((groups, 2 * PACK, SAMPLES), F32),
            pltpu.VMEM((2, WIDTH, pairs * LANES), F32),
            pltpu.VMEM((2, WIDTH, pairs * LANES), F32),
            pltpu.VMEM((2, PIECES, 4 * pairs, GRID + 2 * EDGE, LANES), F32),
            pltpu.SemaphoreType.DMA((len(pieces),)),
        ],
        compiler_params=limit,
        name="window",
    )(*pieces)

    other = shifted(theirs, lambda col, row: (col, row ^ 1))
    sums = lax.all_to_all(sums, axes, 0, 0, tiled=True)

    out = jax.ShapeDtypeStruct(start_field.shape, F32)
    return pl.pallas_call(
        final_kernel,
        out_shape=(out, out),
        in_specs=[anywhere] * 4,
        out_specs=(vmem, vmem),
        scratch_shapes=[
            pltpu.VMEM(sums.shape, F32),
            pltpu.VMEM(mine.shape, F32),
            pltpu.VMEM(mine.shape, F32),
            pltpu.VMEM(start_field.shape, F32),
            pltpu.SemaphoreType.DMA((4,)),
        ],
        compiler_params=small,
        name="final",
    )(sums, mine, other, start_field)


def solution(mesh):
    placed = (
        P(None, "row", "col"),
        P(None, None, "row", "col"),
        P(None, "row", "col"),
        P(None, "row", "col"),
        P(None, None, "row", "col"),
        P(None, "row", "col"),
    )
    return jax.shard_map(
        shards,
        mesh=mesh,
        in_specs=placed,
        out_specs=(P(None, "row", "col"), P(None, "row", "col")),
        check_vma=False,
    )
```

```python
import jax
import jax.numpy as jnp
from jax import lax
from jax.experimental import pallas as pl
from jax.experimental.pallas import tpu as pltpu
from jax.sharding import PartitionSpec as P

GRID = 32
BAND = 4
ITERS = 3
BEND_WEIGHT = 0.05
DAMPING = 0.5

SAMPLES = 256
LANES = 128
PACK = LANES // GRID
TILE_ROWS = 2
HALF_COLS = 4
PIECES = 3
WINDOW_COLS = PIECES * HALF_COLS
WIDTH = WINDOW_COLS * GRID
BLOCK_ROWS = TILE_ROWS * GRID
MASK_ROWS = 8
TABLE_ROWS = 24
TABLES = BLOCK_ROWS + MASK_ROWS
HALF_ROWS = TABLES + HALF_COLS * TABLE_ROWS
BOUNDS = WINDOW_COLS - 1
PLACED = ((0, 1, 10, 11), (4, 5, 6, 7), (8, 9, 2, 3))

LOW, HIGH = 0.5, 6.0
CENTRE, RADIUS = (HIGH + LOW) / 2, (HIGH - LOW) / 2

BASIS = ITERS + 1
PAIRS = [(i, j) for j in range(BASIS) for i in range(min(j, ITERS - 1) + 1)]
SUM_ROWS = 16
SUM_LANES = LANES // SUM_ROWS
EDGE = 8

F32, BF16 = jnp.float32, jnp.bfloat16


def hat(offset):
    return jnp.maximum(1.0 - jnp.abs(offset), 0.0)


def pack_kernel(*refs):
    sources, (own, ahead, back), (*copied, sems) = refs[:6], refs[6:9], refs[9:]
    field, target, rows, band, frac, adjacency = copied
    copies = [
        pltpu.make_async_copy(source, place, sems.at[n]) for n, (source, place) in enumerate(zip(sources, copied))
    ]
    for copy in copies:
        copy.start()
    for copy in copies:
        copy.wait()
    part = lax.axis_index("row") % 2
    not_last_col = (lax.axis_index("col") < lax.axis_size("col") - 1).astype(jnp.int32)
    not_last_row = (lax.axis_index("row") < lax.axis_size("row") - 1).astype(jnp.int32)
    tiles = 2 * HALF_COLS
    sub = lax.broadcasted_iota(jnp.int32, (MASK_ROWS, SAMPLES), 0)
    for half in range(2):
        for comp in range(2):
            own[half, :BLOCK_ROWS, comp * LANES : (comp + 1) * LANES] = field[
                comp, :, half * LANES : (half + 1) * LANES
            ]
    for facing in range(4):
        along = rows[facing].astype(F32) + (frac[facing, 0].astype(F32) + 0.5) / 256.0
        across = band[facing].astype(F32) + (frac[facing, 1].astype(F32) + 0.5) / 256.0
        for tile in range(tiles):
            half, base = tile // HALF_COLS, TABLES + tile % HALF_COLS * TABLE_ROWS + 2 * facing
            lanes = slice(tile * SAMPLES, (tile + 1) * SAMPLES)
            own[half, base : base + 2, :] = along[:, lanes]
            own[half, base + 8 : base + 10, :] = across[:, lanes]
            own[half, base + 16 : base + 18, :] = target[facing // 2, facing % 2][:, lanes]
    place = 2 * sub + lax.broadcasted_iota(jnp.int32, (MASK_ROWS, SAMPLES), 1) // LANES
    for half in range(2):
        masks = jnp.zeros((MASK_ROWS, SAMPLES), F32)
        for tile in range(half * HALF_COLS, (half + 1) * HALF_COLS):
            for side in range(2):
                for row in range(TILE_ROWS):
                    value = adjacency[side, row, tile]
                    if side == 0 and tile == tiles - 1:
                        value = value * not_last_col
                    if side == 1 and row == TILE_ROWS - 1:
                        value = value * not_last_row
                    entry = 4 * (tile % HALF_COLS) + 2 * side + row
                    masks = jnp.where(place == entry, value.astype(F32), masks)
        own[half, BLOCK_ROWS:TABLES, :] = masks
    ahead[...] = own[1 - part]
    back[...] = own[part]


def split(value):
    high = value.astype(BF16)
    return high, (value - high.astype(F32)).astype(BF16)


def position(col):
    for piece, cols in enumerate(PLACED):
        if col in cols:
            return piece * LANES + cols.index(col) * GRID


def pieces_at(step):
    return ((1, 2, 0), (1, 2), (1, 2), (1,))[step]


def groups_of(pairs):
    order, counts = [], []
    for reach in range(ITERS + 1):
        step = ITERS - reach
        for bound in range(step, BOUNDS - step):
            order += [(0, bound, group) for group in range(pairs)]
        for piece in pieces_at(step):
            order += [(1, row, piece) for row in range(4 * pairs - 1)]
        order = list(dict.fromkeys(order))
        counts.append(len(order))
    return order, counts[::-1]


def window_kernel(pairs, *refs):
    count = 4 * pairs
    pieces = refs[:count]
    mine, theirs, sums, slots, vecs, weight_hi, weight_lo, turned_hi, turned_lo, cross, shift, *rest = refs[count:]
    flipped, spread, bends, sems = rest
    order, counts = groups_of(pairs)
    own_pair = pairs // 2
    part = lax.axis_index("row") % 2

    copies = []
    for pair in range(pairs):
        places = (
            slots.at[2 * pair + part, pl.ds(1 - part, 2)],
            slots.at[2 * pair + 1 - part, pl.ds(1 - part, 2)],
            slots.at[2 * pair + part, 2 * part],
            slots.at[2 * pair + 1 - part, 2 * part],
        )
        for kind in range(4):
            at = 4 * pair + kind
            copies.append(pltpu.make_async_copy(pieces[at], places[kind], sems.at[at]))
    for copy in copies:
        copy.start()
    for copy in copies:
        copy.wait()

    sub8 = lax.broadcasted_iota(jnp.int32, (8, LANES), 0)
    lane8 = lax.broadcasted_iota(jnp.int32, (8, LANES), 1)
    near_side = sub8 >= 4
    sub16 = lax.broadcasted_iota(jnp.int32, (16, 2 * LANES), 0)
    lane16 = lax.broadcasted_iota(jnp.int32, (16, 2 * LANES), 1)
    side16 = (lane16 < LANES) == (sub16 % 8 >= 4)
    keep = [
        jnp.where(side16 & (lane16 % LANES // GRID == unit), 1.0, 0.0).astype(BF16)
        for unit in range(PACK)
    ]

    low_lanes = lax.broadcasted_iota(jnp.int32, (BLOCK_ROWS, LANES), 1) < LANES // 2
    for block in range(2 * pairs):
        start = EDGE + block * BLOCK_ROWS
        for comp in range(2):
            left, middle, right = (
                slots[block, piece, :BLOCK_ROWS, comp * LANES : (comp + 1) * LANES] for piece in range(PIECES)
            )
            placed = (jnp.where(low_lanes, left, right), middle, jnp.where(low_lanes, right, left))
            for piece in range(PIECES):
                vecs[0, comp, piece, start : start + BLOCK_ROWS, :] = placed[piece]

    def table(row, col, entry):
        start = TABLES + col % HALF_COLS * TABLE_ROWS + entry
        return slots[row // TILE_ROWS, col // HALF_COLS, start : start + 1, :]

    along_iota = lax.broadcasted_iota(jnp.int32, (GRID, SAMPLES), 0).astype(F32)
    sub_s = lax.broadcasted_iota(jnp.int32, (8, SAMPLES), 0)
    near_s = sub_s >= 4
    depth = jnp.where(near_s, 7 - sub_s, sub_s).astype(F32)

    def set_tables(index, direction, near_tiles, far_tiles):
        hats = []
        for unit in range(PACK):
            both = (near_tiles[unit], far_tiles[unit])
            ys = []
            for side in range(2):
                row, col = both[side]
                entry = 2 * (2 * direction + side) + row % TILE_ROWS
                weight = hat(table(row, col, entry) - along_iota)
                high, low = split(weight)
                start = side * LANES + unit * GRID
                weight_hi[index, start : start + GRID, :] = high
                weight_lo[index, start : start + GRID, :] = low
                hats.append(weight)
                ys.append(table(row, col, 8 + entry))
            row, col = both[0]
            entry = 4 * (col % HALF_COLS) + 2 * direction + row % TILE_ROWS
            at, lane = BLOCK_ROWS + entry // 2, entry % 2 * LANES
            mask = slots[row // TILE_ROWS, col // HALF_COLS, at : at + 1, lane : lane + LANES]
            mask = jnp.concatenate([mask, mask], axis=1)
            signed = jnp.where(near_s, mask, -mask)
            rows = slice(8 * unit, 8 * unit + 8)
            across = hat(jnp.where(near_s, ys[0], ys[1]) - depth) * signed
            cross[index, rows, :] = across
            for comp in range(2):
                shift[index, 2 * unit + comp : 2 * unit + comp + 1, :] = table(
                    row, col, 16 + 4 * direction + 2 * comp + row % TILE_ROWS
                )
        ordered = jnp.concatenate(hats[0::2] + hats[1::2], axis=0).T
        high, low = split(ordered)
        turned_hi[index] = high
        turned_lo[index] = low

    for index, (direction, at, group) in enumerate(order):
        if direction == 0:
            tiles = [(PACK * group + unit, at) for unit in range(PACK)]
            set_tables(index, 0, tiles, [(row, col + 1) for row, col in tiles])
        else:
            tiles = [(at, col) for col in PLACED[group]]
            set_tables(index, 1, tiles, [(row + 1, col) for row, col in tiles])

    spread[...] = jnp.zeros_like(spread)
    bends[...] = jnp.zeros_like(bends)

    def seam_group(index, strips, first):
        half = 8 * 2 * PACK
        high, low = split(jnp.concatenate(strips, axis=0))
        high = jnp.concatenate([high, high], axis=1)
        low = jnp.concatenate([low, low], axis=1)
        left = jnp.concatenate([part * keep[unit] for part in (high, low) for unit in range(PACK)], axis=0)
        both = jnp.dot(left, weight_hi[index], preferred_element_type=F32)
        values = both[:half] + both[half:] + jnp.dot(left[:half], weight_lo[index], preferred_element_type=F32)
        pulled = []
        for unit in range(PACK):
            across = cross[index, 8 * unit : 8 * unit + 8, :]
            for comp in range(2):
                at = 2 * unit + comp
                total = jnp.sum(values[8 * at : 8 * at + 8] * across, axis=0, keepdims=True)
                if first:
                    total = total - shift[index, at : at + 1, :]
                pulled.append(total * across)
        high, low = split(jnp.concatenate(pulled, axis=0))
        both = jnp.dot(jnp.concatenate([high, low], axis=0), turned_hi[index], preferred_element_type=F32)
        back = both[:half] + both[half:] + jnp.dot(high, turned_lo[index], preferred_element_type=F32)
        results = []
        for comp in range(2):
            out = None
            for unit in range(PACK):
                at = 8 * (2 * unit + comp)
                chosen = jnp.where(near_side, back[at : at + 8, :LANES], back[at : at + 8, LANES:])
                out = chosen if out is None else jnp.where(lane8 // GRID == unit, chosen, out)
            results.append(out)
        return results

    sub32 = lax.broadcasted_iota(jnp.int32, (GRID, LANES), 0)
    lane32 = lax.broadcasted_iota(jnp.int32, (GRID, LANES), 1) % GRID
    inner = (sub32 >= 1) & (sub32 <= GRID - 2) & (lane32 >= 1) & (lane32 <= GRID - 2)

    def beside(value):
        return pltpu.roll(value, 1, 1) + pltpu.roll(value, LANES - 1, 1) - 4.0 * value

    def apply(step, scale, own_weight, last_weight):
        for comp in range(2):
            for group in range(pairs):
                for piece in range(PIECES) if step < 2 else (1, 2):
                    start = EDGE + group * LANES
                    flipped[comp, piece * LANES : (piece + 1) * LANES, group * LANES : (group + 1) * LANES] = vecs[
                        step, comp, piece, start : start + LANES, :
                    ].T
        used = order[: counts[step]]

        def place(entry):
            direction, at, group = entry
            lanes = slice(group * LANES, (group + 1) * LANES)
            if direction == 0:
                return True, position(at) + GRID - 8, position(at + 1), lanes
            return False, EDGE + GRID * at + GRID - 8, EDGE + GRID * (at + 1), group

        def take_strips(entry):
            east, before, after, where = place(entry)
            strips = []
            for comp in range(2):
                source = flipped.at[comp, :, where] if east else vecs.at[step, comp, where]
                strips.append(jnp.where(near_side, source[before : before + 8, :], source[after : after + 8, :]))
            return strips

        for index, entry in enumerate(used):
            east, before, after, where = place(entry)
            if east:
                results = seam_group(index, take_strips(entry), step == 0)
                for comp in range(2):
                    result = scale * results[comp]
                    spread[comp, before : before + 8, where] = jnp.where(near_side, result, 0.0)
                    spread[comp, after : after + 8, where] = jnp.where(near_side, 0.0, result)
        for piece in pieces_at(step):
            for comp in range(2):
                for tile in range(4 * pairs):
                    start = EDGE + tile * GRID
                    value = vecs[step, comp, piece, start : start + GRID, :]
                    level = jnp.where(
                        inner,
                        vecs[step, comp, piece, start - 1 : start + GRID - 1, :]
                        + vecs[step, comp, piece, start + 1 : start + GRID + 1, :]
                        + beside(value),
                        0.0,
                    )
                    bends[comp, piece, tile, EDGE : EDGE + GRID, :] = level
                    out = (scale * BEND_WEIGHT) * (
                        bends[comp, piece, tile, EDGE - 1 : EDGE + GRID - 1, :]
                        + bends[comp, piece, tile, EDGE + 1 : EDGE + GRID + 1, :]
                        + beside(level)
                    )
                    if own_weight:
                        out = out + own_weight * value
                    if last_weight:
                        out = out + last_weight * vecs[step - 1, comp, piece, start : start + GRID, :]
                    vecs[step + 1, comp, piece, start : start + GRID, :] = out
        for index, entry in enumerate(used):
            east, before, after, where = place(entry)
            if not east:
                results = seam_group(index, take_strips(entry), step == 0)
                for comp in range(2):
                    result = scale * results[comp]
                    vecs[step + 1, comp, where, before : before + 8, :] += jnp.where(near_side, result, 0.0)
                    vecs[step + 1, comp, where, after : after + 8, :] += jnp.where(near_side, 0.0, result)
        for piece in pieces_at(step):
            for comp in range(2):
                for group in range(pairs):
                    start = EDGE + group * LANES
                    vecs[step + 1, comp, piece, start : start + LANES, :] += spread[
                        comp, piece * LANES : (piece + 1) * LANES, group * LANES : (group + 1) * LANES
                    ].T

    apply(0, -1.0, 0.0, 0.0)
    apply(1, 1.0 / RADIUS, (DAMPING - CENTRE) / RADIUS, 0.0)
    apply(2, 2.0 / RADIUS, 2.0 * (DAMPING - CENTRE) / RADIUS, -1.0)
    first_row = EDGE + own_pair * 2 * BLOCK_ROWS

    def products(pairs_now):
        partial = [jnp.zeros((8, LANES), F32) for _ in pairs_now]
        for comp in range(2):
            for row in range(first_row, first_row + 2 * BLOCK_ROWS, 8):
                values = {k: vecs[1 + k, comp, 1, row : row + 8, :] for k in {k for pair in pairs_now for k in pair}}
                for n, (i, j) in enumerate(pairs_now):
                    partial[n] = partial[n] + values[i] * values[j]
        return partial

    def hand_over(k):
        for comp in range(2):
            for out, block in ((mine, part), (theirs, 1 - part)):
                start = pl.multiple_of(first_row + block * BLOCK_ROWS, EDGE)
                out[k, comp] = vecs[1 + k, comp, 1, pl.ds(start, BLOCK_ROWS), :]

    partial = products([pair for pair in PAIRS if pair[1] < ITERS])
    for k in range(ITERS):
        hand_over(k)
    apply(3, 2.0 / RADIUS, 2.0 * (DAMPING - CENTRE) / RADIUS, -1.0)
    partial += products([pair for pair in PAIRS if pair[1] == ITERS])
    hand_over(ITERS)
    rows = [jnp.sum(value, axis=0, keepdims=True) for value in partial]
    rows.append(jnp.zeros((SUM_ROWS - len(rows), LANES), F32))
    totals = jnp.sum(jnp.concatenate(rows, axis=0), axis=1, keepdims=True)
    slot = lax.broadcasted_iota(jnp.int32, (SUM_ROWS, LANES), 1) // SUM_LANES
    placed = jnp.where(slot == lax.broadcasted_iota(jnp.int32, (SUM_ROWS, LANES), 0), totals, 0.0)
    sums[...] = jnp.broadcast_to(jnp.sum(placed, axis=0, keepdims=True), sums.shape)


def final_kernel(*refs):
    sources, (control, residual), (sums, mine, other, field, sems) = refs[:4], refs[4:6], refs[6:]
    copies = [
        pltpu.make_async_copy(source, target, sems.at[n])
        for n, (source, target) in enumerate(zip(sources, (sums, mine, other, field)))
    ]
    for copy in copies:
        copy.start()
    copies[0].wait()
    part = lax.axis_index("row") % 2
    totals = jnp.sum(sums[...], axis=0, keepdims=True)
    gram = {}
    for n, (i, j) in enumerate(PAIRS):
        gram[i, j] = gram[j, i] = jnp.broadcast_to(totals[:, n * SUM_LANES : n * SUM_LANES + 1], (1, LANES))

    def inner(left, right):
        return sum(
            left[i] * sum(gram[i, j] * right[j] for j in right) for i in left
        )

    def image(vec):
        out = {}

        def add(at, value):
            out[at] = out[at] + value if at in out else value

        for k, value in vec.items():
            add(k, CENTRE * value)
            if k == 0:
                add(1, RADIUS * value)
            else:
                add(k - 1, RADIUS / 2 * value)
                add(k + 1, RADIUS / 2 * value)
        return out

    one = jnp.ones((1, LANES), F32)
    resid, direction, update = {0: one}, {0: one}, {}
    norm = gram[0, 0]
    for iteration in range(ITERS):
        moved = image(direction)
        step = norm / inner(direction, moved)
        for k, value in direction.items():
            update[k] = update[k] + step * value if k in update else step * value
        resid = {k: (resid[k] if k in resid else 0.0) - step * value for k, value in moved.items()}
        if iteration < ITERS - 1:
            after = inner(resid, resid)
            ratio = after / norm
            direction = {k: value + ratio * direction[k] if k in direction else value for k, value in resid.items()}
            norm = after

    for copy in copies[1:]:
        copy.wait()
    for source, half in ((mine, part), (other, 1 - part)):
        lanes = pl.ds(pl.multiple_of(half * LANES, LANES), LANES)
        for comp in range(2):
            basis = [source[k, comp] for k in range(BASIS)]
            control[comp, :, lanes] = field[comp, :, lanes] + sum(update[k] * basis[k] for k in update)
            residual[comp, :, lanes] = sum(resid[k] * basis[k] for k in resid)


def shards(start_field, seam_target, seam_rows, seam_band, seam_frac, adjacency):
    row_count, col_count = lax.axis_size("row"), lax.axis_size("col")
    axes = ("col", "row")
    vmem = pl.BlockSpec(memory_space=pltpu.VMEM)
    anywhere = pl.BlockSpec(memory_space=pl.ANY)
    small = pltpu.CompilerParams(vmem_limit_bytes=4 * 1024 * 1024)

    def shifted(value, move):
        sources = [(col, row) for col in range(col_count) for row in range(row_count)]
        perm = []
        for col, row in sources:
            to_col, to_row = move(col, row)
            if 0 <= to_col < col_count and 0 <= to_row < row_count:
                perm.append((col * row_count + row, to_col * row_count + to_row))
        return lax.ppermute(value, axes, perm)

    half = jax.ShapeDtypeStruct((HALF_ROWS, SAMPLES), F32)
    inputs = (start_field, seam_target, seam_rows, seam_band, seam_frac, adjacency)
    own, ahead, back = pl.pallas_call(
        pack_kernel,
        out_shape=(jax.ShapeDtypeStruct((2, HALF_ROWS, SAMPLES), F32), half, half),
        in_specs=[anywhere] * 6,
        out_specs=(vmem, vmem, vmem),
        scratch_shapes=[pltpu.VMEM(value.shape, value.dtype) for value in inputs[:5]]
        + [pltpu.SMEM(adjacency.shape, adjacency.dtype), pltpu.SemaphoreType.DMA((6,))],
        compiler_params=small,
        name="pack",
    )(*(pltpu.with_memory_space_constraint(value, pltpu.HBM) for value in inputs))

    outward = lambda row: 1 - 2 * (row % 2)
    pieces = (
        own,
        shifted(own, lambda col, row: (col, row ^ 1)),
        shifted(ahead, lambda col, row: (col + outward(row), row)),
        shifted(back, lambda col, row: (col - outward(row), row ^ 1)),
    )
    if row_count > 2:
        from_above = [shifted(piece, lambda col, row: (col, row + 2)) for piece in pieces]
        from_below = [shifted(piece, lambda col, row: (col, row - 2)) for piece in pieces]
        pieces = (*from_above, *pieces, *from_below)
    pairs = len(pieces) // 4
    groups = len(groups_of(pairs)[0])
    limit = pltpu.CompilerParams(vmem_limit_bytes=(groups * 11 // 20 + 8 * pairs + 1) * 1024 * 1024)

    part_shape = jax.ShapeDtypeStruct((BASIS, 2, BLOCK_ROWS, LANES), F32)
    mine, theirs, sums = pl.pallas_call(
        lambda *refs: window_kernel(pairs, *refs),
        out_shape=(part_shape, part_shape, jax.ShapeDtypeStruct((row_count * col_count, LANES), F32)),
        in_specs=[anywhere] * len(pieces),
        out_specs=(vmem, vmem, vmem),
        scratch_shapes=[
            pltpu.VMEM((2 * pairs, PIECES, HALF_ROWS, SAMPLES), F32),
            pltpu.VMEM((BASIS + 1, 2, PIECES, 4 * pairs * GRID + 2 * EDGE, LANES), F32),
            pltpu.VMEM((groups, 2 * LANES, SAMPLES), BF16),
            pltpu.VMEM((groups, 2 * LANES, SAMPLES), BF16),
            pltpu.VMEM((groups, SAMPLES, 2 * LANES), BF16),
            pltpu.VMEM((groups, SAMPLES, 2 * LANES), BF16),
            pltpu.VMEM((groups, 8 * PACK, SAMPLES), F32),
            pltpu.VMEM((groups, 2 * PACK, SAMPLES), F32),
            pltpu.VMEM((2, WIDTH, pairs * LANES), F32),
            pltpu.VMEM((2, WIDTH, pairs * LANES), F32),
            pltpu.VMEM((2, PIECES, 4 * pairs, GRID + 2 * EDGE, LANES), F32),
            pltpu.SemaphoreType.DMA((len(pieces),)),
        ],
        compiler_params=limit,
        name="window",
    )(*pieces)

    other = shifted(theirs, lambda col, row: (col, row ^ 1))
    sums = lax.all_to_all(sums, axes, 0, 0, tiled=True)

    out = jax.ShapeDtypeStruct(start_field.shape, F32)
    return pl.pallas_call(
        final_kernel,
        out_shape=(out, out),
        in_specs=[anywhere] * 4,
        out_specs=(vmem, vmem),
        scratch_shapes=[
            pltpu.VMEM(sums.shape, F32),
            pltpu.VMEM(mine.shape, F32),
            pltpu.VMEM(mine.shape, F32),
            pltpu.VMEM(start_field.shape, F32),
            pltpu.SemaphoreType.DMA((4,)),
        ],
        compiler_params=small,
        name="final",
    )(sums, mine, other, start_field)


def solution(mesh):
    placed = (
        P(None, "row", "col"),
        P(None, None, "row", "col"),
        P(None, "row", "col"),
        P(None, "row", "col"),
        P(None, None, "row", "col"),
        P(None, "row", "col"),
    )
    return jax.shard_map(
        shards,
        mesh=mesh,
        in_specs=placed,
        out_specs=(P(None, "row", "col"), P(None, "row", "col")),
        check_vma=False,
    )
```
